32 devices in a mesh: groups: 2 (over y), strip: 4 (over z), slab: 2 (over x), sub: 2 (over core).
Axes of the slice: x: 2, y: 2, z: 4, core: 2. Of those that a mesh axis runs over, the one named last changes fastest.
Arguments:
- features: bfloat16 [8, 2, 2, 12, 8, 8, 512], P(('groups', 'strip'), 'sub', 'slab'), parts along dimension 0, may hold values from -6 to 6
- voxel_mask: int32 [8, 2, 2, 12, 8, 8, 8], P(('groups', 'strip'), 'sub', 'slab'), parts along dimension 0, may hold values 0 or 1
- block_pos: int32 [8, 2, 2, 12], P(('groups', 'strip'), 'sub', 'slab'), parts along dimension 0, may hold values from 0 to 16, as said below
- conv_weight: bfloat16 [3, 3, 3, 64, 64], replicated, may hold values from -0.21875 to 0.21875
- conv_gain: float32 [64], replicated, may hold values from 0.25 to 1.75
- conv_bias: float32 [64], replicated, may hold values from -1.2 to 1.2
- height_weight: bfloat16 [2048, 128], P('slab'), may hold values from -0.375 to 0.375
- height_bias: float32 [128], replicated, may hold values from -1.2 to 1.2
- bev_weight: bfloat16 [3, 3, 128, 256], replicated, may hold values from -0.25 to 0.25
- bev_gain: float32 [256], replicated, may hold values from 0.25 to 1.75
- bev_bias: float32 [256], replicated, may hold values from -1.2 to 1.2
- head_weight: bfloat16 [256, 11], replicated, may hold values from -0.5 to 0.5
- head_bias: float32 [11], replicated, may hold values from -2 to 2
Outputs:
- head_maps: float32 [64, 128, 11], P(('groups', 'strip', 'slab'), 'sub'), parts along dimension 0
The draws below stay inside these ranges and needn't reach their ends.
There are 2 independent parts, one for each index of `groups`. The reference program is written for one: setup_inputs(seed, part) draws one part's arguments, and reference() takes and returns one part's arrays. A program takes and returns all parts, laid end to end along the dimension named above; an argument that names none is the same for every part. Nothing has to cross between parts.
Inputs may be any that keep to these rules, and one draw needn't show every extreme that they name: `block_pos`: on each device the live slots name distinct positions below 16; the empty ones hold 16. In every draw some device has all 12 slots live.
All inputs are finite; a program needn't handle non-finite values. No bound on the sum of `voxel_mask` on one device may be relied on, other than what follows from the above.
Results may differ from the reference program's by a relative error of at most 0.0041.
Values may be sent and summed in bfloat16 or wider, within the bound.
A program may use at most 128 MiB of HBM per device.

```python
import jax
import jax.numpy as jnp
from jax import lax

C = 64
CB = 128
CH = 256
HEADS = 11
EDGE = 8
BY_DEV = 8
BZ_DEV = 2
SLOTS = 12
XV = 32
YV = 128
ZV = 32
N_STRIP = 4
N_SLAB = 2
N_SUB = 2


def draw_block_pos(key, part):
    key = jax.random.fold_in(key, 11)
    positions = BY_DEV * BZ_DEV
    grid_shape = (N_STRIP, N_SUB, N_SLAB)
    device_count = N_STRIP * N_SUB * N_SLAB
    key_count, key_full, key_order, key_shuffle = jax.random.split(key, 4)
    raw_draw = jax.random.randint(key_count, grid_shape, 0, SLOTS)
    counts = jnp.minimum(SLOTS, jnp.maximum(1, SLOTS // 4 + raw_draw * raw_draw // SLOTS))
    full_device = jax.random.randint(key_full, (), 0, device_count)
    counts = jnp.where(jnp.arange(device_count).reshape(grid_shape) == full_device, SLOTS, counts)
    scores = jax.random.randint(key_order, grid_shape + (positions,), 0, 2 ** 20) * positions + jnp.arange(positions)
    chosen = jnp.argsort(scores, axis=-1)[..., :SLOTS]
    live_slot = jnp.arange(SLOTS) < counts[..., None]
    picked = jnp.where(live_slot, chosen, positions)
    mixing = jax.random.randint(key_shuffle, grid_shape + (SLOTS,), 0, 2 ** 20) * SLOTS + jnp.arange(SLOTS)
    shuffle = jnp.argsort(mixing, axis=-1)
    return jnp.take_along_axis(picked, shuffle, axis=-1).astype(jnp.int32)


def set_ends(values, stream_key, low, largest):
    longest = values.shape.index(max(values.shape))
    spots = []
    for shift in (0, 1):
        where = [jax.random.randint(jax.random.fold_in(stream_key, axis), (), 0, length) for axis, length in enumerate(values.shape)]
        where[longest] = (where[longest] + shift) % values.shape[longest]
        spots.append(tuple(where))
    return values.at[spots[0]].set(low).at[spots[1]].set(largest)


def level_of(stream_key, shape, cuts, least, top_value):
    def one(axis_at, shards_of):
        steps = jax.random.uniform(jax.random.fold_in(jax.random.fold_in(stream_key, 6), axis_at), (shards_of,), jnp.float32, least / len(cuts), top_value / len(cuts))
        return jnp.repeat(jnp.exp(steps), shape[axis_at] // shards_of).reshape((-1,) + (1,) * (len(shape) - axis_at - 1))

    factor_of = one(*cuts[0])
    for cut in cuts[1:]:
        factor_of = factor_of * one(*cut)
    return factor_of


def scatter_about(own_key, shape, deviation, most, pieces=(), kind=jnp.bfloat16):
    result = deviation * jax.random.normal(own_key, shape, jnp.float32)
    if pieces:
        result = result * level_of(own_key, shape, pieces, -0.22, 0.18)
    return jnp.clip(result, -most, most).astype(kind)


def setup_inputs(seed: int = 0, part: int = 0) -> dict:
    key_list = jax.random.split(jax.random.key(seed), 14)
    own_keys = jax.random.split(jax.random.fold_in(key_list[13], part), 14)
    features = scatter_about(own_keys[0], (N_STRIP, N_SUB, N_SLAB, SLOTS, EDGE, EDGE, EDGE * C), 1.0, 6.0, ((0, 4), (1, 2), (2, 2)))
    voxel_mask = set_ends((jax.random.randint(own_keys[1], (N_STRIP, N_SUB, N_SLAB, SLOTS, EDGE, EDGE, EDGE), 0, 16) < 15).astype(jnp.int32), jax.random.fold_in(own_keys[1], 1), 0, 1)
    block_pos = draw_block_pos(jax.random.fold_in(jax.random.fold_in(key_list[13], part), 71), part)
    conv_weight = scatter_about(key_list[3], (3, 3, 3, C, C), (27 * C // 2) ** -0.5, 0.21875)
    conv_gain = jnp.clip(1.0 + 0.15 * jax.random.normal(key_list[4], (C,), jnp.float32), 0.25, 1.75)
    conv_bias = scatter_about(key_list[5], (C,), 0.3, 1.2, (), jnp.float32)
    height_weight = scatter_about(key_list[6], (ZV * C, CB), (ZV * C // 8) ** -0.5, 0.375, ((0, 2),))
    height_bias = scatter_about(key_list[7], (CB,), 0.3, 1.2, (), jnp.float32)
    bev_weight = scatter_about(key_list[8], (3, 3, CB, CH), (9 * CB // 2) ** -0.5, 0.25)
    bev_gain = jnp.clip(1.0 + 0.15 * jax.random.normal(key_list[9], (CH,), jnp.float32), 0.25, 1.75)
    bev_bias = scatter_about(key_list[10], (CH,), 0.3, 1.2, (), jnp.float32)
    head_weight = scatter_about(key_list[11], (CH, HEADS), (CH // 2) ** -0.5, 0.5)
    head_bias = scatter_about(key_list[12], (HEADS,), 0.5, 2.0, (), jnp.float32)
    return {"features": features, "voxel_mask": voxel_mask, "block_pos": block_pos, "conv_weight": conv_weight, "conv_gain": conv_gain, "conv_bias": conv_bias, "height_weight": height_weight, "height_bias": height_bias, "bev_weight": bev_weight, "bev_gain": bev_gain, "bev_bias": bev_bias, "head_weight": head_weight, "head_bias": head_bias}


def place_blocks(blocks, places):
    table = jnp.zeros((BY_DEV * BZ_DEV + 1,) + blocks.shape[1:], blocks.dtype)
    return table.at[places].set(blocks)[:BY_DEV * BZ_DEV]


def to_grid(blocks, flat_places):
    device_count = N_STRIP * N_SUB * N_SLAB
    flat_blocks = blocks.reshape((device_count,) + blocks.shape[3:])
    tables = jax.vmap(place_blocks)(flat_blocks, flat_places)
    tables = tables.reshape(N_STRIP, N_SUB, N_SLAB, BY_DEV, BZ_DEV, EDGE, EDGE, EDGE * C)
    return tables.transpose(0, 5, 1, 3, 6, 2, 4, 7).reshape(XV, YV, ZV * C)


def reference(features, voxel_mask, block_pos, conv_weight, conv_gain, conv_bias, height_weight, height_bias, bev_weight, bev_gain, bev_bias, head_weight, head_bias):
    device_count = N_STRIP * N_SUB * N_SLAB
    live_mask = voxel_mask.astype(jnp.bfloat16)
    wide_mask = jnp.broadcast_to(live_mask[..., None], live_mask.shape + (C,)).reshape(features.shape)
    masked = features * wide_mask
    flat_places = block_pos.reshape(device_count, SLOTS)
    grid = to_grid(masked, flat_places)
    padded = jnp.pad(grid, ((1, 1), (1, 1), (C, C)))
    kernel = conv_weight.astype(jnp.float32)
    flat_mask = voxel_mask.reshape(device_count, SLOTS, EDGE, EDGE, EDGE).astype(jnp.float32)

    def device_conv(inputs):
        device, places, masks = inputs
        strip_at = device // (N_SUB * N_SLAB)
        sub_at = (device // N_SLAB) % N_SUB
        slab_at = device % N_SLAB
        block_y = jnp.minimum(places // BZ_DEV, BY_DEV - 1)
        block_z = places % BZ_DEV

        def cut_window(one_y, one_z):
            starts = ((strip_at * EDGE).astype(jnp.int32), ((sub_at * BY_DEV + one_y) * EDGE).astype(jnp.int32), ((slab_at * BZ_DEV + one_z) * EDGE * C).astype(jnp.int32))
            return lax.dynamic_slice(padded, starts, (EDGE + 2, EDGE + 2, (EDGE + 2) * C))

        windows = jax.vmap(cut_window)(block_y, block_z).astype(jnp.float32).reshape(SLOTS, EDGE + 2, EDGE + 2, EDGE + 2, C)
        totals = jnp.zeros((SLOTS, EDGE, EDGE, EDGE, C), jnp.float32)
        for shift_x in range(3):
            for shift_y in range(3):
                for shift_z in range(3):
                    sliced = windows[:, shift_x:shift_x + EDGE, shift_y:shift_y + EDGE, shift_z:shift_z + EDGE, :]
                    totals = totals + jnp.einsum("nxyzc,cd->nxyzd", sliced, kernel[shift_x, shift_y, shift_z])
        activated = jax.nn.relu(totals * conv_gain + conv_bias) * masks[..., None]
        return activated.astype(jnp.bfloat16).reshape(SLOTS, EDGE, EDGE, EDGE * C)

    activated = lax.map(device_conv, (jnp.arange(device_count, dtype=jnp.int32), flat_places, flat_mask))
    voxel_features = to_grid(activated.reshape(features.shape), flat_places)
    height_full = height_weight.astype(jnp.float32)

    def compress(row_block):
        return jnp.dot(row_block.astype(jnp.float32), height_full)

    column_sums = lax.map(compress, voxel_features)
    bev = jax.nn.relu(column_sums + height_bias).astype(jnp.bfloat16)
    bev_pad = jnp.pad(bev, ((1, 1), (1, 1), (0, 0))).astype(jnp.float32)
    bev_kernel = bev_weight.astype(jnp.float32)
    bev_pre = jnp.zeros((XV, YV, CH), jnp.float32)
    for shift_x in range(3):
        for shift_y in range(3):
            bev_pre = bev_pre + jnp.einsum("xyc,cd->xyd", bev_pad[shift_x:shift_x + XV, shift_y:shift_y + YV], bev_kernel[shift_x, shift_y])
    hidden = jax.nn.relu(bev_pre * bev_gain + bev_bias).astype(jnp.bfloat16)
    return jnp.einsum("xyc,cd->xyd", hidden.astype(jnp.float32), head_weight.astype(jnp.float32)) + head_bias
```

```python
import jax
import jax.numpy as jnp
from jax import lax
from jax.experimental import pallas as pl
from jax.experimental.pallas import tpu as pltpu
from jax.sharding import PartitionSpec as P

BY_DEV = 8
BZ_DEV = 2
MESH = pl.DeviceIdType.MESH
F32 = jnp.float32
BF16 = jnp.bfloat16

DIRS = [(a, b) for a in (-1, 0, 1) for b in (-1, 0, 1) if (a, b) != (0, 0)]


def body(
    sizes,
    pos_ref,
    feat_ref,
    mask_ref,
    cw_ref,
    gain_ref,
    bias_ref,
    hw_ref,
    hb_ref,
    bw_ref,
    bgain_ref,
    bbias_ref,
    head_ref,
    headb_ref,
    out_ref,
    xbuf,
    xm,
    xp,
    ybuf,
    wide,
    mbuf,
    band,
    part,
    edge,
    rbuf,
    cbuf,
    hcol,
    bexp,
    face_send,
    face_recv,
    y_send,
    y_recv,
    sum_send,
    sum_recv,
    col_send,
    col_recv,
):
    n_strip, n_slab, n_sub = sizes
    share = 8 // n_slab
    s = lax.axis_index("strip")
    l = lax.axis_index("slab")
    u = lax.axis_index("sub")

    barrier = pltpu.get_barrier_semaphore()
    for a in (-1, 0, 1):

        @pl.when((s + a >= 0) & (s + a < n_strip))
        def _():
            for dl in range(n_slab):
                for du in range(n_sub):
                    if a == 0 and dl == 0 and du == 0:
                        continue
                    pl.semaphore_signal(
                        barrier,
                        inc=1,
                        device_id={
                            "strip": s + a,
                            "slab": lax.rem(l + dl, n_slab),
                            "sub": lax.rem(u + du, n_sub),
                        },
                        device_id_type=MESH,
                    )

    chan_of = lax.broadcasted_iota(jnp.int32, (8, 512), 1) // 64
    level_of = lax.broadcasted_iota(jnp.int32, (8, 512), 0)
    spread = (chan_of == level_of).astype(F32).astype(BF16)
    wide[...] = jnp.dot(
        mask_ref[...].reshape(12 * 64, 8).astype(F32).astype(BF16),
        spread,
        preferred_element_type=F32,
    ).reshape(12, 64, 512)

    def slot_at(place):
        slot = jnp.int32(0)
        live = jnp.int32(0)
        for t in range(12):
            hit = pos_ref[t] == place
            slot = jnp.where(hit, t, slot)
            live = jnp.where(hit, 1, live)
        return slot, live.astype(F32)

    for pz in range(BZ_DEV):
        for pair in range(BY_DEV // 2):
            masks, blocks = [], []
            for half in range(2):
                slot, live = slot_at((2 * pair + half) * BZ_DEV + pz)
                mask = wide[slot] * live
                masks.append(mask.reshape(8, 8, 512))
                blocks.append((feat_ref[slot].astype(F32) * mask).reshape(8, 8, 512))
            rows = pl.ds(16 * pair, 16)
            mbuf[:, rows, pl.ds(512 * pz, 512)] = jnp.concatenate(masks, axis=1).astype(BF16)
            xbuf[pl.ds(1, 8), rows, pl.ds(128 + 512 * pz, 512)] = jnp.concatenate(
                blocks, axis=1
            ).astype(BF16)

    @pl.when(s == 0)
    def _():
        xbuf[0] = jnp.zeros((64, 1280), BF16)

    @pl.when(s == n_strip - 1)
    def _():
        xbuf[9] = jnp.zeros((64, 1280), BF16)

    for edge_row, at_edge in ((0, s > 0), (9, s < n_strip - 1)):

        @pl.when(at_edge & (l == 0))
        def _():
            xbuf[edge_row, :, pl.ds(0, 128)] = jnp.zeros((64, 128), BF16)

        @pl.when(at_edge & (l == n_slab - 1))
        def _():
            xbuf[edge_row, :, pl.ds(1152, 128)] = jnp.zeros((64, 128), BF16)

    @pl.when(l == 0)
    def _():
        xbuf[pl.ds(1, 8), :, pl.ds(0, 128)] = jnp.zeros((8, 64, 128), BF16)

    @pl.when(l == n_slab - 1)
    def _():
        xbuf[pl.ds(1, 8), :, pl.ds(1152, 128)] = jnp.zeros((8, 64, 128), BF16)

    @pl.when(u == 0)
    def _():
        ybuf[0] = jnp.zeros((10, 16, 1280), BF16)

    @pl.when(u == n_sub - 1)
    def _():
        ybuf[1] = jnp.zeros((10, 16, 1280), BF16)

    strips_near = (s > 0).astype(jnp.int32) + (s < n_strip - 1).astype(jnp.int32) + 1
    pl.semaphore_wait(barrier, strips_near * (n_slab * n_sub) - 1)

    def exists(a, b):
        return (s + a >= 0) & (s + a < n_strip) & (l + b >= 0) & (l + b < n_slab)

    def face_copy(at):
        a, b = DIRS[at]
        src_x, dst_x = {-1: ((1, 1), (9, 1)), 0: ((1, 8), (1, 8)), 1: ((8, 1), (0, 1))}[a]
        src_z, dst_z = {
            -1: ((128, 128), (1152, 128)),
            0: ((128, 1024), (128, 1024)),
            1: ((1024, 128), (0, 128)),
        }[b]
        return pltpu.make_async_remote_copy(
            src_ref=xbuf.at[pl.ds(*src_x), :, pl.ds(*src_z)],
            dst_ref=xbuf.at[pl.ds(*dst_x), :, pl.ds(*dst_z)],
            send_sem=face_send.at[at],
            recv_sem=face_recv.at[at],
            device_id={"strip": s + a, "slab": l + b},
            device_id_type=MESH,
        )

    for at, (a, b) in enumerate(DIRS):

        @pl.when(exists(a, b))
        def _():
            face_copy(at).start()

    def make_band(tap, carry):
        blank = jnp.zeros((64, 64), BF16)
        taps = [cw_ref[3 * tap + k] for k in range(3)]
        for e in range(8):
            cols = [taps[e - o - 1] if 0 <= e - o - 1 <= 2 else blank for o in range(4)]
            band[tap, pl.ds(64 * e, 64), :] = jnp.concatenate(cols, axis=1)
        return carry

    lax.fori_loop(0, 9, make_band, 0)

    for at, (a, b) in enumerate(DIRS):

        @pl.when(exists(-a, -b))
        def _():
            face_copy(at).wait_recv()

    def y_copy(side):
        start = 48 if side == 0 else 0
        return pltpu.make_async_remote_copy(
            src_ref=xbuf.at[:, pl.ds(start, 16), :],
            dst_ref=ybuf.at[side],
            send_sem=y_send.at[side],
            recv_sem=y_recv.at[side],
            device_id={"sub": u + 1 if side == 0 else u - 1},
            device_id_type=MESH,
        )

    @pl.when(u < n_sub - 1)
    def _():
        y_copy(0).start()

    @pl.when(u > 0)
    def _():
        y_copy(1).start()

    @pl.when(u > 0)
    def _():
        y_copy(0).wait_recv()

    @pl.when(u < n_sub - 1)
    def _():
        y_copy(1).wait_recv()

    def shift_rows(x, carry):
        rows = xbuf[x].astype(F32)
        row_at = lax.broadcasted_iota(jnp.int32, rows.shape, 0)
        before = ybuf[0, x].astype(F32)[15:16]
        after = ybuf[1, x].astype(F32)[0:1]
        xm[x] = jnp.where(row_at == 0, before, pltpu.roll(rows, 1, 0)).astype(BF16)
        xp[x] = jnp.where(row_at == 63, after, pltpu.roll(rows, 63, 0)).astype(BF16)
        return carry

    lax.fori_loop(0, 10, shift_rows, 0)

    gain4 = jnp.concatenate([gain_ref[...]] * 4, axis=1)
    bias4 = jnp.concatenate([bias_ref[...]] * 4, axis=1)
    part[...] = jnp.zeros_like(part)

    def conv_group(j, carry):
        low = pl.multiple_of(256 * j, 256)
        acc = jnp.zeros((512, 256), F32)
        for dx in range(3):
            for dy, source in enumerate((xm, xbuf, xp)):
                window = source[pl.ds(dx, 8), :, pl.ds(low, 512)].reshape(512, 512)
                acc = acc + jnp.dot(window, band[3 * dx + dy], preferred_element_type=F32)
        mask = mbuf[:, :, pl.ds(low, 256)].reshape(512, 256).astype(F32)
        voxels = (jnp.maximum(acc * gain4 + bias4, 0.0) * mask).astype(BF16)
        sums = jnp.dot(voxels, hw_ref[pl.ds(low, 256), :], preferred_element_type=F32)
        part[...] += sums.reshape(8, 64, 128)
        return carry

    lax.fori_loop(0, 4, conv_group, 0)

    edge[0] = part[:, 56:64, :][:, 7, :]
    edge[1] = part[:, 0:8, :][:, 0, :]

    def row_copy(target, rows, at_row, a, sem, source):
        return pltpu.make_async_remote_copy(
            src_ref=part.at[pl.ds(rows[0], rows[1])],
            dst_ref=rbuf.at[source, pl.ds(at_row, rows[1])],
            send_sem=sum_send.at[sem],
            recv_sem=sum_recv.at[source + n_slab * (a + 1)],
            device_id={"strip": s + a, "slab": target},
            device_id_type=MESH,
        )

    def slab_copy(target, source):
        low = max(0, target * share - 1)
        high = min(8, target * share + share + 1)
        return row_copy(target, (low, high - low), low - (target * share - 1), 0, target, source)

    def up_copy(source):
        return row_copy(0, (7, 1), 0, 1, n_slab, source)

    def down_copy(source):
        return row_copy(n_slab - 1, (0, 1), share + 1, -1, n_slab + 1, source)

    def col_copy(side, a, target, source):
        return pltpu.make_async_remote_copy(
            src_ref=edge.at[side],
            dst_ref=cbuf.at[side, source, pl.ds(8 * (1 - a), 8)],
            send_sem=col_send.at[side, a + 1, target],
            recv_sem=col_recv.at[side, a + 1, source],
            device_id={
                "strip": s + a,
                "slab": target,
                "sub": u + 1 if side == 0 else u - 1,
            },
            device_id_type=MESH,
        )

    has_up = s < n_strip - 1
    has_down = s > 0
    sub_to = (u < n_sub - 1, u > 0)
    sub_from = (u > 0, u < n_sub - 1)
    for t in range(n_slab):

        @pl.when(l != t)
        def _():
            slab_copy(t, l).start()

    @pl.when(has_up)
    def _():
        up_copy(l).start()

    @pl.when(has_down)
    def _():
        down_copy(l).start()

    for side in range(2):

        @pl.when(sub_to[side])
        def _():
            for t in range(n_slab):
                col_copy(side, 0, t, l).start()

        @pl.when(sub_to[side] & has_up)
        def _():
            col_copy(side, 1, 0, l).start()

        @pl.when(sub_to[side] & has_down)
        def _():
            col_copy(side, -1, n_slab - 1, l).start()

    for t in range(n_slab):

        @pl.when(l == t)
        def _():
            low = max(0, t * share - 1)
            high = min(8, t * share + share + 1)
            rbuf[t, pl.ds(low - (t * share - 1), high - low)] = part[pl.ds(low, high - low)]
            for source in range(n_slab):
                if source != t:
                    slab_copy(t, source).wait_recv()

    @pl.when((l == 0) & has_down)
    def _():
        for source in range(n_slab):
            up_copy(source).wait_recv()

    @pl.when((l == 0) & (s == 0))
    def _():
        rbuf[:, pl.ds(0, 1)] = jnp.zeros((n_slab, 1, 64, 128), F32)

    @pl.when((l == n_slab - 1) & has_up)
    def _():
        for source in range(n_slab):
            down_copy(source).wait_recv()

    @pl.when((l == n_slab - 1) & (s == n_strip - 1))
    def _():
        rbuf[:, pl.ds(share + 1, 1)] = jnp.zeros((n_slab, 1, 64, 128), F32)

    for side in range(2):

        @pl.when(sub_from[side])
        def _():
            for source in range(n_slab):
                col_copy(side, 0, 0, source).wait_recv()

        @pl.when(sub_from[side] & (l == 0) & has_down)
        def _():
            for source in range(n_slab):
                col_copy(side, 1, 0, source).wait_recv()

        @pl.when(sub_from[side] & (l == n_slab - 1) & has_up)
        def _():
            for source in range(n_slab):
                col_copy(side, -1, 0, source).wait_recv()

        @pl.when(jnp.logical_not(sub_from[side]))
        def _():
            cbuf[side] = jnp.zeros((n_slab, 24, 128), F32)

        @pl.when(sub_from[side] & jnp.logical_not((l == 0) & has_down))
        def _():
            cbuf[side, :, pl.ds(0, 8)] = jnp.zeros((n_slab, 8, 128), F32)

        @pl.when(sub_from[side] & jnp.logical_not((l == n_slab - 1) & has_up))
        def _():
            cbuf[side, :, pl.ds(16, 8)] = jnp.zeros((n_slab, 8, 128), F32)

    hb = hb_ref[...]
    first_x = s * 8 + l * share - 1

    col_x = lax.broadcasted_iota(jnp.int32, (24, 128), 0) + (s * 8 - 8)
    for side in range(2):
        col = cbuf[side, 0]
        for source in range(1, n_slab):
            col = col + cbuf[side, source]
        inside = (col_x >= 0) & (col_x < 8 * n_strip) & sub_from[side]
        hcol[side] = jnp.where(inside, jnp.maximum(col + hb, 0.0), 0.0)

    for i in range(share + 2):
        total = rbuf[0, i]
        for source in range(1, n_slab):
            total = total + rbuf[source, i]
        total = jnp.maximum(total + hb, 0.0)
        if i == 0 or i == share + 1:
            row_ok = (first_x + i >= 0) & (first_x + i < 8 * n_strip)
            total = jnp.where(row_ok, total, 0.0)
        row_at = lax.broadcasted_iota(jnp.int32, total.shape, 0)
        before = hcol[0, pl.ds(7 + l * share + i, 1), :]
        after = hcol[1, pl.ds(7 + l * share + i, 1), :]
        bexp[i, :, pl.ds(0, 128)] = jnp.where(row_at == 0, before, pltpu.roll(total, 1, 0)).astype(
            BF16
        )
        bexp[i, :, pl.ds(128, 128)] = total.astype(BF16)
        bexp[i, :, pl.ds(256, 128)] = jnp.where(row_at == 63, after, pltpu.roll(total, 63, 0)).astype(
            BF16
        )

    pre = jnp.zeros((share * 64, bw_ref.shape[2]), F32)
    for dx in range(3):
        pre = pre + jnp.dot(
            bexp[pl.ds(dx, share)].reshape(share * 64, 384), bw_ref[dx], preferred_element_type=F32
        )
    hidden = jnp.maximum(pre * bgain_ref[...] + bbias_ref[...], 0.0).astype(BF16)
    out_ref[...] = jnp.dot(hidden, head_ref[...], preferred_element_type=F32) + headb_ref[...]

    for at, (a, b) in enumerate(DIRS):

        @pl.when(exists(a, b))
        def _():
            face_copy(at).wait_send()

    for side in range(2):

        @pl.when(sub_to[side])
        def _():
            y_copy(side).wait_send()
            for t in range(n_slab):
                col_copy(side, 0, t, l).wait_send()

        @pl.when(sub_to[side] & has_up)
        def _():
            col_copy(side, 1, 0, l).wait_send()

        @pl.when(sub_to[side] & has_down)
        def _():
            col_copy(side, -1, n_slab - 1, l).wait_send()

    for t in range(n_slab):

        @pl.when(l != t)
        def _():
            slab_copy(t, l).wait_send()

    @pl.when(has_up)
    def _():
        up_copy(l).wait_send()

    @pl.when(has_down)
    def _():
        down_copy(l).wait_send()


def solution(mesh):
    n_strip, n_slab, n_sub = mesh.shape["strip"], mesh.shape["slab"], mesh.shape["sub"]
    share = 8 // n_slab

    def on_device(
        features,
        voxel_mask,
        block_pos,
        conv_weight,
        conv_gain,
        conv_bias,
        height_weight,
        height_bias,
        bev_weight,
        bev_gain,
        bev_bias,
        head_weight,
        head_bias,
    ):
        heads = head_weight.shape[1]
        chan_out = bev_weight.shape[3]
        vmem = pl.BlockSpec(memory_space=pltpu.VMEM)
        out = pl.pallas_call(
            lambda *refs: body((n_strip, n_slab, n_sub), *refs),
            out_shape=jax.ShapeDtypeStruct((share * 64, heads), F32),
            in_specs=[pl.BlockSpec(memory_space=pltpu.SMEM)] + [vmem] * 12,
            out_specs=vmem,
            scratch_shapes=[
                pltpu.VMEM((10, 64, 1280), BF16),
                pltpu.VMEM((10, 64, 1280), BF16),
                pltpu.VMEM((10, 64, 1280), BF16),
                pltpu.VMEM((2, 10, 16, 1280), BF16),
                pltpu.VMEM((12, 64, 512), F32),
                pltpu.VMEM((8, 64, 1024), BF16),
                pltpu.VMEM((9, 512, 256), BF16),
                pltpu.VMEM((8, 64, 128), F32),
                pltpu.VMEM((2, 8, 128), F32),
                pltpu.VMEM((n_slab, share + 2, 64, 128), F32),
                pltpu.VMEM((2, n_slab, 24, 128), F32),
                pltpu.VMEM((2, 24, 128), F32),
                pltpu.VMEM((share + 2, 64, 384), BF16),
                pltpu.SemaphoreType.DMA((8,)),
                pltpu.SemaphoreType.DMA((8,)),
                pltpu.SemaphoreType.DMA((2,)),
                pltpu.SemaphoreType.DMA((2,)),
                pltpu.SemaphoreType.DMA((n_slab + 2,)),
                pltpu.SemaphoreType.DMA((3 * n_slab,)),
                pltpu.SemaphoreType.DMA((2, 3, n_slab)),
                pltpu.SemaphoreType.DMA((2, 3, n_slab)),
            ],
            compiler_params=pltpu.CompilerParams(
                collective_id=0, has_side_effects=True, vmem_limit_bytes=48 * 2**20
            ),
        )(
            block_pos.reshape(12),
            features.reshape(12, 64, 512),
            voxel_mask.reshape(12, 64, 8),
            conv_weight.reshape(27, 64, 64),
            conv_gain.reshape(1, -1),
            conv_bias.reshape(1, -1),
            height_weight,
            height_bias.reshape(1, -1),
            bev_weight.reshape(3, -1, chan_out),
            bev_gain.reshape(1, -1),
            bev_bias.reshape(1, -1),
            head_weight,
            head_bias.reshape(1, -1),
        )
        return out.reshape(share, 64, heads)

    in_specs = (
        P(("groups", "strip"), "sub", "slab", None, None, None, None),
        P(("groups", "strip"), "sub", "slab", None, None, None, None),
        P(("groups", "strip"), "sub", "slab", None),
        P(),
        P(),
        P(),
        P("slab", None),
        P(),
        P(),
        P(),
        P(),
        P(),
        P(),
    )
    out_specs = P(("groups", "strip", "slab"), "sub", None)
    return jax.shard_map(
        on_device, mesh=mesh, in_specs=in_specs, out_specs=out_specs, check_vma=False
    )
```

```python
import jax
import jax.numpy as jnp
from jax import lax
from jax.experimental import pallas as pl
from jax.experimental.pallas import tpu as pltpu
from jax.sharding import PartitionSpec as P

BY_DEV = 8
BZ_DEV = 2
MESH = pl.DeviceIdType.MESH
F32 = jnp.float32
BF16 = jnp.bfloat16

DIRS = [(a, b) for a in (-1, 0, 1) for b in (-1, 0, 1) if (a, b) != (0, 0)]
Y_DIRS = [(0, 0)] + DIRS


def body(
    sizes,
    pos_ref,
    feat_hbm,
    mask_hbm,
    posv_hbm,
    cw_hbm,
    gain_hbm,
    bias_hbm,
    hw_hbm,
    hb_hbm,
    bw_hbm,
    bgain_hbm,
    bbias_hbm,
    head_hbm,
    headb_hbm,
    out_ref,
    feat_ref,
    mask_ref,
    posv_ref,
    cw_ref,
    gain_ref,
    bias_ref,
    hw_ref,
    hb_ref,
    bw_ref,
    bgain_ref,
    bbias_ref,
    head_ref,
    headb_ref,
    xbuf,
    xm,
    xp,
    ybuf,
    wide,
    mbuf,
    band,
    part,
    partb,
    edge,
    rbuf,
    cbuf,
    hcol,
    bexp,
    in_sem,
    face_send,
    face_recv,
    y_send,
    y_recv,
    sum_send,
    sum_recv,
    low_send,
    low_recv,
    high_send,
    high_recv,
    col_send,
    col_recv,
):
    n_strip, n_slab, n_sub = sizes
    share = 8 // n_slab
    s = lax.axis_index("strip")
    l = lax.axis_index("slab")
    u = lax.axis_index("sub")

    fetched = (
        (posv_hbm, posv_ref),
        (mask_hbm, mask_ref),
        (feat_hbm, feat_ref),
        (cw_hbm, cw_ref),
        (gain_hbm, gain_ref),
        (bias_hbm, bias_ref),
        (hw_hbm, hw_ref),
        (hb_hbm, hb_ref),
        (bw_hbm, bw_ref),
        (bgain_hbm, bgain_ref),
        (bbias_hbm, bbias_ref),
        (head_hbm, head_ref),
        (headb_hbm, headb_ref),
    )
    fetches = [
        pltpu.make_async_copy(src, dst, in_sem.at[at]) for at, (src, dst) in enumerate(fetched)
    ]
    for fetch in fetches:
        fetch.start()

    xbuf[0] = jnp.zeros((64, 1280), BF16)
    xbuf[9] = jnp.zeros((64, 1280), BF16)
    xbuf[pl.ds(1, 8), :, pl.ds(0, 128)] = jnp.zeros((8, 64, 128), BF16)
    xbuf[pl.ds(1, 8), :, pl.ds(1152, 128)] = jnp.zeros((8, 64, 128), BF16)
    ybuf[...] = jnp.zeros(ybuf.shape, BF16)
    rbuf[...] = jnp.zeros(rbuf.shape, BF16)
    cbuf[...] = jnp.zeros(cbuf.shape, F32)
    part[...] = jnp.zeros(part.shape, F32)

    barrier = pltpu.get_barrier_semaphore()
    for a in (-1, 0, 1):

        @pl.when((s + a >= 0) & (s + a < n_strip))
        def _():
            for dl in range(n_slab):
                for du in range(n_sub):
                    if a == 0 and dl == 0 and du == 0:
                        continue
                    pl.semaphore_signal(
                        barrier,
                        inc=1,
                        device_id={
                            "strip": s + a,
                            "slab": lax.rem(l + dl, n_slab),
                            "sub": lax.rem(u + du, n_sub),
                        },
                        device_id_type=MESH,
                    )

    level_of = lax.rem(lax.broadcasted_iota(jnp.int32, (512, 512), 0), 8)
    chan_of = lax.broadcasted_iota(jnp.int32, (512, 512), 1) // 64
    spread = (level_of == chan_of).astype(F32).astype(BF16)
    own_col = lax.broadcasted_iota(jnp.int32, (64, 512), 1) // 8
    keep = (own_col == lax.broadcasted_iota(jnp.int32, (64, 512), 0)).astype(F32)
    fetches[0].wait()
    fetches[1].wait()
    places = lax.broadcasted_iota(jnp.int32, (16, 12), 0)
    pick = (places == posv_ref[...]).astype(F32).astype(BF16)
    by_place = lax.dot_general(
        pick,
        mask_ref[...].astype(F32).astype(BF16),
        (((1,), (1,)), ((), ())),
        preferred_element_type=F32,
    )
    rows_of = jnp.concatenate([(by_place[p : p + 1] * keep).astype(BF16) for p in range(16)], axis=0)
    wide[...] = jnp.dot(rows_of, spread, preferred_element_type=F32).reshape(16, 64, 512)

    def slot_at(place):
        slot = jnp.int32(0)
        for t in range(12):
            slot = jnp.where(pos_ref[t] == place, t, slot)
        return slot

    fetches[2].wait()
    for pz in range(BZ_DEV):
        for pair in range(BY_DEV // 2):
            masks, blocks = [], []
            for half in range(2):
                place = (2 * pair + half) * BZ_DEV + pz
                mask = wide[place]
                masks.append(mask.reshape(8, 8, 512))
                blocks.append((feat_ref[slot_at(place)].astype(F32) * mask).reshape(8, 8, 512))
            rows = pl.ds(16 * pair, 16)
            mbuf[:, rows, pl.ds(512 * pz, 512)] = jnp.concatenate(masks, axis=1).astype(BF16)
            xbuf[pl.ds(1, 8), rows, pl.ds(128 + 512 * pz, 512)] = jnp.concatenate(
                blocks, axis=1
            ).astype(BF16)

    strips_near = (s > 0).astype(jnp.int32) + (s < n_strip - 1).astype(jnp.int32) + 1
    pl.semaphore_wait(barrier, strips_near * (n_slab * n_sub) - 1)

    def exists(a, b):
        return (s + a >= 0) & (s + a < n_strip) & (l + b >= 0) & (l + b < n_slab)

    sub_to = (u < n_sub - 1, u > 0)
    sub_from = (u > 0, u < n_sub - 1)

    def ranges(a, b):
        src_x, dst_x = {-1: ((1, 1), (9, 1)), 0: ((1, 8), (1, 8)), 1: ((8, 1), (0, 1))}[a]
        src_z, dst_z = {
            -1: ((128, 128), (1152, 128)),
            0: ((128, 1024), (128, 1024)),
            1: ((1024, 128), (0, 128)),
        }[b]
        return pl.ds(*src_x), pl.ds(*dst_x), pl.ds(*src_z), pl.ds(*dst_z)

    def face_copy(at):
        a, b = DIRS[at]
        src_x, dst_x, src_z, dst_z = ranges(a, b)
        return pltpu.make_async_remote_copy(
            src_ref=xbuf.at[src_x, :, src_z],
            dst_ref=xbuf.at[dst_x, :, dst_z],
            send_sem=face_send.at[at],
            recv_sem=face_recv.at[at],
            device_id={"strip": s + a, "slab": l + b},
            device_id_type=MESH,
        )

    def y_copy(side, at):
        a, b = Y_DIRS[at]
        src_x, dst_x, src_z, dst_z = ranges(a, b)
        return pltpu.make_async_remote_copy(
            src_ref=xbuf.at[src_x, pl.ds(48 if side == 0 else 0, 16), src_z],
            dst_ref=ybuf.at[side, dst_x, :, dst_z],
            send_sem=y_send.at[side, at],
            recv_sem=y_recv.at[side, at],
            device_id={
                "strip": s + a,
                "slab": l + b,
                "sub": u + 1 if side == 0 else u - 1,
            },
            device_id_type=MESH,
        )

    for side in range(2):

        @pl.when(sub_to[side])
        def _():
            y_copy(side, 0).start()

    for at, (a, b) in enumerate(DIRS):

        @pl.when(exists(a, b))
        def _():
            face_copy(at).start()
            for side in range(2):

                @pl.when(sub_to[side])
                def _():
                    y_copy(side, at + 1).start()

    fetches[3].wait()

    def make_band(tap, carry):
        blank = jnp.zeros((64, 64), BF16)
        taps = [cw_ref[3 * tap + k] for k in range(3)]
        for e in range(8):
            cols = [taps[e - o - 1] if 0 <= e - o - 1 <= 2 else blank for o in range(4)]
            band[tap, pl.ds(64 * e, 64), :] = jnp.concatenate(cols, axis=1)
        return carry

    lax.fori_loop(0, 9, make_band, 0)

    for fetch in fetches[4:]:
        fetch.wait()

    for side in range(2):

        @pl.when(sub_from[side])
        def _():
            y_copy(side, 0).wait_recv()

    def shift_rows(x, low, width):
        lanes = pl.ds(low, width)
        rows = xbuf[x, :, lanes].astype(F32)
        row_at = lax.broadcasted_iota(jnp.int32, rows.shape, 0)
        before = ybuf[0, x, :, lanes].astype(F32)[15:16]
        after = ybuf[1, x, :, lanes].astype(F32)[0:1]
        xm[x, :, lanes] = jnp.where(row_at == 0, before, pltpu.roll(rows, 1, 0)).astype(BF16)
        xp[x, :, lanes] = jnp.where(row_at == 63, after, pltpu.roll(rows, 63, 0)).astype(BF16)

    def shift_own(x, carry):
        shift_rows(x, 128, 1024)
        return carry

    lax.fori_loop(1, 9, shift_own, 0)

    gain4 = jnp.concatenate([gain_ref[...]] * 4, axis=1)
    bias4 = jnp.concatenate([bias_ref[...]] * 4, axis=1)

    def conv(j, x, count):
        low = pl.multiple_of(256 * j, 256)
        acc = jnp.zeros((count * 64, 256), F32)
        for dx in range(3):
            for dy, source in enumerate((xm, xbuf, xp)):
                window = source[pl.ds(x + dx, count), :, pl.ds(low, 512)].reshape(count * 64, 512)
                acc = acc + jnp.dot(window, band[3 * dx + dy], preferred_element_type=F32)
        mask = mbuf[pl.ds(x, count), :, pl.ds(low, 256)].reshape(count * 64, 256).astype(F32)
        voxels = (jnp.maximum(acc * gain4 + bias4, 0.0) * mask).astype(BF16)
        sums = jnp.dot(voxels, hw_ref[pl.ds(low, 256), :], preferred_element_type=F32)
        part[pl.ds(x + 1, count)] += sums.reshape(count, 64, 128)

    def conv_inner(j, carry):
        conv(j, 1, 6)
        return carry

    lax.fori_loop(1, 3, conv_inner, 0)

    for at, (a, b) in enumerate(DIRS):

        @pl.when(exists(-a, -b))
        def _():
            face_copy(at).wait_recv()
            for side in range(2):

                @pl.when(sub_from[side])
                def _():
                    y_copy(side, at + 1).wait_recv()

    def shift_ends(at, carry):
        shift_rows(9 * at, 0, 1280)
        return carry

    lax.fori_loop(0, 2, shift_ends, 0)

    def shift_rims(x, carry):
        shift_rows(x, 0, 128)
        shift_rows(x, 1152, 128)
        return carry

    lax.fori_loop(1, 9, shift_rims, 0)

    mine = l // (n_slab // 2)

    def conv_half(half):
        def conv_outer(at, carry):
            conv(3 * at, 4 * half, 4)
            return carry

        def conv_end(j, carry):
            conv(j, 7 * half, 1)
            return carry

        lax.fori_loop(0, 2, conv_outer, 0)
        lax.fori_loop(1, 3, conv_end, 0)
        partb[pl.ds(4 * half, 4)] = part[pl.ds(4 * half + 1, 4)].astype(BF16)

    def sum_copy(target, source):
        return pltpu.make_async_remote_copy(
            src_ref=partb.at[pl.ds(target * share, share)],
            dst_ref=rbuf.at[source, pl.ds(1, share)],
            send_sem=sum_send.at[target],
            recv_sem=sum_recv.at[source],
            device_id={"slab": target},
            device_id_type=MESH,
        )

    def low_copy(target, a, source):
        return pltpu.make_async_remote_copy(
            src_ref=partb.at[pl.ds(7 if a else target * share - 1, 1)],
            dst_ref=rbuf.at[source, pl.ds(0, 1)],
            send_sem=low_send.at[target],
            recv_sem=low_recv.at[source],
            device_id={"strip": s + a, "slab": target},
            device_id_type=MESH,
        )

    def high_copy(target, a, source):
        return pltpu.make_async_remote_copy(
            src_ref=partb.at[pl.ds(0 if a else target * share + share, 1)],
            dst_ref=rbuf.at[source, pl.ds(share + 1, 1)],
            send_sem=high_send.at[target],
            recv_sem=high_recv.at[source],
            device_id={"strip": s + a, "slab": target},
            device_id_type=MESH,
        )

    def col_copy(side, a, target, source):
        return pltpu.make_async_remote_copy(
            src_ref=edge.at[side],
            dst_ref=cbuf.at[side, source, pl.ds(8 * (1 - a), 8)],
            send_sem=col_send.at[side, a + 1, target],
            recv_sem=col_recv.at[side, a + 1, source],
            device_id={
                "strip": s + a,
                "slab": target,
                "sub": u + 1 if side == 0 else u - 1,
            },
            device_id_type=MESH,
        )

    has_up = s < n_strip - 1
    has_down = s > 0
    last = n_slab - 1

    conv_half(1 - mine)
    for t in range(n_slab):

        @pl.when(t // (n_slab // 2) != mine)
        def _():
            sum_copy(t, l).start()

    conv_half(mine)

    edge[0] = part[pl.ds(1, 8), 56:64, :][:, 7, :]
    edge[1] = part[pl.ds(1, 8), 0:8, :][:, 0, :]

    for t in range(n_slab):

        @pl.when((l != t) & (t // (n_slab // 2) == mine))
        def _():
            sum_copy(t, l).start()

        if t > 0:

            @pl.when(l != t)
            def _():
                low_copy(t, 0, l).start()

        if t < last:

            @pl.when(l != t)
            def _():
                high_copy(t, 0, l).start()

    @pl.when(has_up)
    def _():
        low_copy(0, 1, l).start()

    @pl.when(has_down)
    def _():
        high_copy(last, -1, l).start()

    for side in range(2):

        @pl.when(sub_to[side])
        def _():
            for t in range(n_slab):
                col_copy(side, 0, t, l).start()

        @pl.when(sub_to[side] & has_up)
        def _():
            col_copy(side, 1, 0, l).start()

        @pl.when(sub_to[side] & has_down)
        def _():
            col_copy(side, -1, last, l).start()

    for source in range(n_slab):

        @pl.when(l != source)
        def _():
            sum_copy(0, source).wait_recv()

        @pl.when(((l > 0) & (l != source)) | ((l == 0) & has_down))
        def _():
            low_copy(0, 1, source).wait_recv()

        @pl.when(((l < last) & (l != source)) | ((l == last) & has_up))
        def _():
            high_copy(0, -1, source).wait_recv()

        for side in range(2):

            @pl.when(sub_from[side])
            def _():
                col_copy(side, 0, 0, source).wait_recv()

            @pl.when(sub_from[side] & (l == 0) & has_down)
            def _():
                col_copy(side, 1, 0, source).wait_recv()

            @pl.when(sub_from[side] & (l == last) & has_up)
            def _():
                col_copy(side, -1, 0, source).wait_recv()

    hb = hb_ref[...]
    first_x = s * 8 + l * share - 1

    col_x = lax.broadcasted_iota(jnp.int32, (24, 128), 0) + (s * 8 - 8)
    for side in range(2):
        col = cbuf[side, 0]
        for source in range(1, n_slab):
            col = col + cbuf[side, source]
        inside = (col_x >= 0) & (col_x < 8 * n_strip) & sub_from[side]
        hcol[side] = jnp.where(inside, jnp.maximum(col + hb, 0.0), 0.0)

    for i in range(share + 2):
        total = part[l * share + i]
        for source in range(n_slab):
            total = total + rbuf[source, i].astype(F32)
        total = jnp.maximum(total + hb, 0.0)
        if i == 0 or i == share + 1:
            row_ok = (first_x + i >= 0) & (first_x + i < 8 * n_strip)
            total = jnp.where(row_ok, total, 0.0)
        row_at = lax.broadcasted_iota(jnp.int32, total.shape, 0)
        before = hcol[0, pl.ds(7 + l * share + i, 1), :]
        after = hcol[1, pl.ds(7 + l * share + i, 1), :]
        bexp[i, :, pl.ds(0, 128)] = jnp.where(row_at == 0, before, pltpu.roll(total, 1, 0)).astype(
            BF16
        )
        bexp[i, :, pl.ds(128, 128)] = total.astype(BF16)
        bexp[i, :, pl.ds(256, 128)] = jnp.where(row_at == 63, after, pltpu.roll(total, 63, 0)).astype(
            BF16
        )

    pre = jnp.zeros((share * 64, bw_ref.shape[2]), F32)
    for dx in range(3):
        pre = pre + jnp.dot(
            bexp[pl.ds(dx, share)].reshape(share * 64, 384), bw_ref[dx], preferred_element_type=F32
        )
    hidden = jnp.maximum(pre * bgain_ref[...] + bbias_ref[...], 0.0).astype(BF16)
    maps = lax.dot_general(
        head_ref[...], hidden, (((1,), (1,)), ((), ())), preferred_element_type=F32
    )
    maps = maps + jnp.transpose(jnp.broadcast_to(headb_ref[...], (8, headb_ref.shape[1])))[:, 0:1]
    for i in range(share):
        out_ref[:, i, :] = maps[:, 64 * i : 64 * i + 64]

    for at, (a, b) in enumerate(DIRS):

        @pl.when(exists(a, b))
        def _():
            face_copy(at).wait_send()
            for side in range(2):

                @pl.when(sub_to[side])
                def _():
                    y_copy(side, at + 1).wait_send()

    for side in range(2):

        @pl.when(sub_to[side])
        def _():
            y_copy(side, 0).wait_send()
            for t in range(n_slab):
                col_copy(side, 0, t, l).wait_send()

        @pl.when(sub_to[side] & has_up)
        def _():
            col_copy(side, 1, 0, l).wait_send()

        @pl.when(sub_to[side] & has_down)
        def _():
            col_copy(side, -1, last, l).wait_send()

    for t in range(n_slab):

        @pl.when(l != t)
        def _():
            sum_copy(t, l).wait_send()
            if t > 0:
                low_copy(t, 0, l).wait_send()
            if t < last:
                high_copy(t, 0, l).wait_send()

    @pl.when(has_up)
    def _():
        low_copy(0, 1, l).wait_send()

    @pl.when(has_down)
    def _():
        high_copy(last, -1, l).wait_send()


def solution(mesh):
    n_strip, n_slab, n_sub = mesh.shape["strip"], mesh.shape["slab"], mesh.shape["sub"]
    share = 8 // n_slab

    def on_device(
        features,
        voxel_mask,
        block_pos,
        conv_weight,
        conv_gain,
        conv_bias,
        height_weight,
        height_bias,
        bev_weight,
        bev_gain,
        bev_bias,
        head_weight,
        head_bias,
    ):
        heads = head_weight.shape[1]
        chan_out = bev_weight.shape[3]
        vmem = pl.BlockSpec(memory_space=pltpu.VMEM)
        far = pl.BlockSpec(memory_space=pl.ANY)
        places = block_pos.reshape(12)
        operands = (
            features.reshape(12, 64, 512),
            voxel_mask.reshape(12, 8, 8, 8).transpose(1, 2, 3, 0).reshape(512, 12),
            places.reshape(1, 12),
            conv_weight.reshape(27, 64, 64),
            conv_gain.reshape(1, -1),
            conv_bias.reshape(1, -1),
            height_weight,
            height_bias.reshape(1, -1),
            bev_weight.reshape(3, -1, chan_out),
            bev_gain.reshape(1, -1),
            bev_bias.reshape(1, -1),
            head_weight.T,
            head_bias.reshape(1, -1),
        )
        out = pl.pallas_call(
            lambda *refs: body((n_strip, n_slab, n_sub), *refs),
            out_shape=jax.ShapeDtypeStruct((heads, share, 64), F32),
            in_specs=[pl.BlockSpec(memory_space=pltpu.SMEM)] + [far] * 13,
            out_specs=vmem,
            scratch_shapes=[pltpu.VMEM(each.shape, each.dtype) for each in operands]
            + [
                pltpu.VMEM((10, 64, 1280), BF16),
                pltpu.VMEM((10, 64, 1280), BF16),
                pltpu.VMEM((10, 64, 1280), BF16),
                pltpu.VMEM((2, 10, 16, 1280), BF16),
                pltpu.VMEM((16, 64, 512), F32),
                pltpu.VMEM((8, 64, 1024), BF16),
                pltpu.VMEM((9, 512, 256), BF16),
                pltpu.VMEM((10, 64, 128), F32),
                pltpu.VMEM((8, 64, 128), BF16),
                pltpu.VMEM((2, 8, 128), F32),
                pltpu.VMEM((n_slab, share + 2, 64, 128), BF16),
                pltpu.VMEM((2, n_slab, 24, 128), F32),
                pltpu.VMEM((2, 24, 128), F32),
                pltpu.VMEM((share + 2, 64, 384), BF16),
                pltpu.SemaphoreType.DMA((13,)),
                pltpu.SemaphoreType.DMA((8,)),
                pltpu.SemaphoreType.DMA((8,)),
                pltpu.SemaphoreType.DMA((2, 9)),
                pltpu.SemaphoreType.DMA((2, 9)),
            ]
            + [pltpu.SemaphoreType.DMA((n_slab,))] * 6
            + [pltpu.SemaphoreType.DMA((2, 3, n_slab))] * 2,
            compiler_params=pltpu.CompilerParams(
                collective_id=0, has_side_effects=True, vmem_limit_bytes=60 * 2**20
            ),
        )(places, *operands)
        return out.transpose(1, 2, 0)

    in_specs = (
        P(("groups", "strip"), "sub", "slab", None, None, None, None),
        P(("groups", "strip"), "sub", "slab", None, None, None, None),
        P(("groups", "strip"), "sub", "slab", None),
        P(),
        P(),
        P(),
        P("slab", None),
        P(),
        P(),
        P(),
        P(),
        P(),
        P(),
    )
    out_specs = P(("groups", "strip", "slab"), "sub", None)
    return jax.shard_map(
        on_device, mesh=mesh, in_specs=in_specs, out_specs=out_specs, check_vma=False
    )
```

```python
import jax
import jax.numpy as jnp
from jax import lax
from jax.experimental import pallas as pl
from jax.experimental.pallas import tpu as pltpu
from jax.sharding import PartitionSpec as P

BY_DEV = 8
BZ_DEV = 2
MESH = pl.DeviceIdType.MESH
F32 = jnp.float32
BF16 = jnp.bfloat16

DIRS = [(a, b) for a in (-1, 0, 1) for b in (-1, 0, 1) if (a, b) != (0, 0)]
Y_DIRS = [(0, 0)] + DIRS


def body(
    sizes,
    pos_ref,
    feat_hbm,
    mask_hbm,
    posv_hbm,
    cw_hbm,
    gain_hbm,
    bias_hbm,
    hw_hbm,
    hb_hbm,
    bw_hbm,
    bgain_hbm,
    bbias_hbm,
    head_hbm,
    headb_hbm,
    out_ref,
    feat_ref,
    mask_ref,
    posv_ref,
    cw_ref,
    gain_ref,
    bias_ref,
    hw_ref,
    hb_ref,
    bw_ref,
    bgain_ref,
    bbias_ref,
    head_ref,
    headb_ref,
    xbuf,
    xm,
    xp,
    ybuf,
    wide,
    mbuf,
    band,
    zband,
    zbuf,
    zm,
    zp,
    accb,
    part,
    edge,
    rbuf,
    cbuf,
    hcol,
    bexp,
    in_sem,
    face_send,
    face_recv,
    y_send,
    y_recv,
    sum_send,
    sum_recv,
    low_send,
    low_recv,
    high_send,
    high_recv,
    col_send,
    col_recv,
):
    n_strip, n_slab, n_sub = sizes
    share = 8 // n_slab
    s = lax.axis_index("strip")
    l = lax.axis_index("slab")
    u = lax.axis_index("sub")

    fetched = (
        (posv_hbm, posv_ref),
        (mask_hbm, mask_ref),
        (feat_hbm, feat_ref),
        (cw_hbm, cw_ref),
        (gain_hbm, gain_ref),
        (bias_hbm, bias_ref),
        (hw_hbm, hw_ref),
        (hb_hbm, hb_ref),
        (bw_hbm, bw_ref),
        (bgain_hbm, bgain_ref),
        (bbias_hbm, bbias_ref),
        (head_hbm, head_ref),
        (headb_hbm, headb_ref),
    )
    fetches = [
        pltpu.make_async_copy(src, dst, in_sem.at[at]) for at, (src, dst) in enumerate(fetched)
    ]
    for fetch in fetches:
        fetch.start()

    for side in (0, 9, 10, 11):
        xbuf[side] = jnp.zeros((64, 1280), BF16)
        xm[side] = jnp.zeros((64, 1280), BF16)
        xp[side] = jnp.zeros((64, 1280), BF16)
    for low in (0, 1152):
        for each in (xm, xp):
            each[pl.ds(1, 8), :, pl.ds(low, 128)] = jnp.zeros((8, 64, 128), BF16)
    xbuf[pl.ds(1, 8), :, pl.ds(0, 128)] = jnp.zeros((8, 64, 128), BF16)
    xbuf[pl.ds(1, 8), :, pl.ds(1152, 128)] = jnp.zeros((8, 64, 128), BF16)
    ybuf[...] = jnp.zeros(ybuf.shape, BF16)
    rbuf[...] = jnp.zeros(rbuf.shape, F32)
    zbuf[...] = jnp.zeros(zbuf.shape, BF16)
    cbuf[...] = jnp.zeros(cbuf.shape, F32)
    part[...] = jnp.zeros(part.shape, F32)

    barrier = pltpu.get_barrier_semaphore()
    for a in (-1, 0, 1):

        @pl.when((s + a >= 0) & (s + a < n_strip))
        def _():
            for dl in range(n_slab):
                for du in range(n_sub):
                    if a == 0 and dl == 0 and du == 0:
                        continue
                    pl.semaphore_signal(
                        barrier,
                        inc=1,
                        device_id={
                            "strip": s + a,
                            "slab": lax.rem(l + dl, n_slab),
                            "sub": lax.rem(u + du, n_sub),
                        },
                        device_id_type=MESH,
                    )

    level_of = lax.rem(lax.broadcasted_iota(jnp.int32, (512, 512), 0), 8)
    chan_of = lax.broadcasted_iota(jnp.int32, (512, 512), 1) // 64
    spread = (level_of == chan_of).astype(F32).astype(BF16)
    own_col = lax.broadcasted_iota(jnp.int32, (64, 512), 1) // 8
    keep = (own_col == lax.broadcasted_iota(jnp.int32, (64, 512), 0)).astype(F32)
    fetches[0].wait()
    fetches[1].wait()
    places = lax.broadcasted_iota(jnp.int32, (16, 12), 0)
    pick = (places == posv_ref[...]).astype(F32).astype(BF16)
    by_place = lax.dot_general(
        pick,
        mask_ref[...].astype(F32).astype(BF16),
        (((1,), (1,)), ((), ())),
        preferred_element_type=F32,
    )
    rows_of = jnp.concatenate([(by_place[p : p + 1] * keep).astype(BF16) for p in range(16)], axis=0)
    wide[...] = jnp.dot(rows_of, spread, preferred_element_type=F32).reshape(16, 64, 512)

    def slot_at(place):
        slot = jnp.int32(0)
        for t in range(12):
            slot = jnp.where(pos_ref[t] == place, t, slot)
        return slot

    fetches[2].wait()
    for pz in range(BZ_DEV):
        for pair in range(BY_DEV // 2):
            masks, blocks = [], []
            for half in range(2):
                place = (2 * pair + half) * BZ_DEV + pz
                mask = wide[place]
                masks.append(mask.reshape(8, 8, 512))
                blocks.append((feat_ref[slot_at(place)].astype(F32) * mask).reshape(8, 8, 512))
            rows = pl.ds(16 * pair, 16)
            mbuf[:, rows, pl.ds(512 * pz, 512)] = jnp.concatenate(masks, axis=1).astype(BF16)
            xbuf[pl.ds(1, 8), rows, pl.ds(128 + 512 * pz, 512)] = jnp.concatenate(
                blocks, axis=1
            ).astype(BF16)

    fetches[3].wait()

    def make_band(tap, carry):
        blank = jnp.zeros((64, 64), BF16)
        taps = [cw_ref[3 * tap + k] for k in range(3)]
        for e in range(8):
            cols = [taps[e - o - 1] if 0 <= e - o - 1 <= 2 else blank for o in range(4)]
            band[tap, pl.ds(64 * e, 64), :] = jnp.concatenate(cols, axis=1)
        low = jnp.concatenate([taps[0], blank], axis=1)
        high = jnp.concatenate([blank, taps[2]], axis=1)
        empty = jnp.zeros((64, 128), BF16)
        for e, rim in enumerate((empty, low, high, empty)):
            zband[tap, pl.ds(64 * e, 64), :] = rim
        return carry

    lax.fori_loop(0, 9, make_band, 0)

    def conv_own(j, sources):
        low = pl.multiple_of(256 * j, 256)
        acc = jnp.zeros((512, 256), F32)
        for dx in range(3):
            for dy, source in sources:
                window = source[pl.ds(dx, 8), :, pl.ds(low, 512)].reshape(512, 512)
                acc = acc + jnp.dot(window, band[3 * dx + dy], preferred_element_type=F32)
        return acc.reshape(8, 64, 256)

    def conv_middle(j, carry):
        accb[j] = conv_own(j, ((1, xbuf),))
        return carry

    def conv_sides(j, carry):
        accb[j] += conv_own(j, ((0, xm), (2, xp)))
        return carry

    lax.fori_loop(0, 2, conv_middle, 0)

    strips_near = (s > 0).astype(jnp.int32) + (s < n_strip - 1).astype(jnp.int32) + 1
    pl.semaphore_wait(barrier, strips_near * (n_slab * n_sub) - 1)

    def exists(a, b):
        return (s + a >= 0) & (s + a < n_strip) & (l + b >= 0) & (l + b < n_slab)

    sub_to = (u < n_sub - 1, u > 0)
    sub_from = (u > 0, u < n_sub - 1)

    def ranges(a, b):
        src_x, dst_x = {-1: ((1, 1), (9, 1)), 0: ((1, 8), (1, 8)), 1: ((8, 1), (0, 1))}[a]
        src_z, dst_z = {
            -1: ((128, 128), (1152, 128)),
            0: ((128, 1024), (128, 1024)),
            1: ((1024, 128), (0, 128)),
        }[b]
        return pl.ds(*src_x), pl.ds(*dst_x), pl.ds(*src_z), pl.ds(*dst_z)

    def face_copy(at):
        a, b = DIRS[at]
        src_x, dst_x, src_z, dst_z = ranges(a, b)
        if b == 0:
            target = xbuf.at[pl.ds(11 if a < 0 else 10, 1), :, dst_z]
        else:
            target = zbuf.at[dst_x, :, pl.ds(128 if b < 0 else 0, 128)]
        return pltpu.make_async_remote_copy(
            src_ref=xbuf.at[src_x, :, src_z],
            dst_ref=target,
            send_sem=face_send.at[at],
            recv_sem=face_recv.at[at],
            device_id={"strip": s + a, "slab": l + b},
            device_id_type=MESH,
        )

    def y_copy(side, at):
        a, b = Y_DIRS[at]
        src_x, dst_x, src_z, dst_z = ranges(a, b)
        return pltpu.make_async_remote_copy(
            src_ref=xbuf.at[src_x, pl.ds(48 if side == 0 else 0, 16), src_z],
            dst_ref=ybuf.at[side, dst_x, :, dst_z],
            send_sem=y_send.at[side, at],
            recv_sem=y_recv.at[side, at],
            device_id={
                "strip": s + a,
                "slab": l + b,
                "sub": u + 1 if side == 0 else u - 1,
            },
            device_id_type=MESH,
        )

    for side in range(2):

        @pl.when(sub_to[side])
        def _():
            y_copy(side, 0).start()

    for at, (a, b) in enumerate(DIRS):

        @pl.when(exists(a, b))
        def _():
            face_copy(at).start()
            for side in range(2):

                @pl.when(sub_to[side])
                def _():
                    y_copy(side, at + 1).start()

    lax.fori_loop(2, 4, conv_middle, 0)

    for fetch in fetches[4:]:
        fetch.wait()

    for side in range(2):

        @pl.when(sub_from[side])
        def _():
            y_copy(side, 0).wait_recv()

    def shift_rows(x, low, width):
        lanes = pl.ds(low, width)
        rows = xbuf[x, :, lanes].astype(F32)
        row_at = lax.broadcasted_iota(jnp.int32, rows.shape, 0)
        before = ybuf[0, x, :, lanes].astype(F32)[15:16]
        after = ybuf[1, x, :, lanes].astype(F32)[0:1]
        xm[x, :, lanes] = jnp.where(row_at == 0, before, pltpu.roll(rows, 1, 0)).astype(BF16)
        xp[x, :, lanes] = jnp.where(row_at == 63, after, pltpu.roll(rows, 63, 0)).astype(BF16)

    def shift_own(x, carry):
        shift_rows(x, 128, 1024)
        return carry

    lax.fori_loop(1, 9, shift_own, 0)

    gain4 = jnp.concatenate([gain_ref[...]] * 4, axis=1)
    bias4 = jnp.concatenate([bias_ref[...]] * 4, axis=1)

    lax.fori_loop(0, 4, conv_sides, 0)

    for at, (a, b) in enumerate(DIRS):

        @pl.when(exists(-a, -b))
        def _():
            face_copy(at).wait_recv()
            for side in range(2):

                @pl.when(sub_from[side])
                def _():
                    y_copy(side, at + 1).wait_recv()

    def shifted(rows, before, after):
        row_at = lax.broadcasted_iota(jnp.int32, rows.shape, 0)
        up = jnp.where(row_at == 0, before, pltpu.roll(rows, 1, 0)).astype(BF16)
        down = jnp.where(row_at == 63, after, pltpu.roll(rows, 63, 0)).astype(BF16)
        return up, down

    def shift_ends(at, carry):
        lanes = pl.ds(128, 1024)
        xm[10 + at, :, lanes], xp[10 + at, :, lanes] = shifted(
            xbuf[10 + at, :, lanes].astype(F32),
            ybuf[0, 9 * at, :, lanes].astype(F32)[15:16],
            ybuf[1, 9 * at, :, lanes].astype(F32)[0:1],
        )
        return carry

    lax.fori_loop(0, 2, shift_ends, 0)

    def shift_rims(x, carry):
        before, after = [
            jnp.concatenate(
                [ybuf[side, x, :, pl.ds(low, 128)].astype(F32) for low in (0, 1152)], axis=1
            )
            for side in range(2)
        ]
        zm[x], zp[x] = shifted(zbuf[x].astype(F32), before[15:16], after[0:1])
        return carry

    lax.fori_loop(0, 10, shift_rims, 0)

    mine = l // (n_slab // 2)

    def conv_half(half):
        beyond = jnp.zeros((256, 256), F32)
        for dy, source in enumerate((xm, xbuf, xp)):
            window = jnp.concatenate([source[10 + half, :, pl.ds(256 * j, 512)] for j in range(4)], axis=0)
            beyond = beyond + jnp.dot(window, band[6 * half + dy], preferred_element_type=F32)
        accb[:, 7 * half] += beyond.reshape(4, 64, 256)
        rims = jnp.zeros((256, 128), F32)
        for dx in range(3):
            for dy, source in enumerate((zm, zbuf, zp)):
                window = source[pl.ds(4 * half + dx, 4)].reshape(256, 256)
                rims = rims + jnp.dot(window, zband[3 * dx + dy], preferred_element_type=F32)
        lane = lax.broadcasted_iota(jnp.int32, rims.shape, 1)
        none = jnp.zeros_like(rims)
        sums = jnp.zeros((256, 128), F32)
        for j in range(4):
            acc = accb[j, pl.ds(4 * half, 4)].reshape(256, 256)
            if j == 0:
                acc = acc + jnp.concatenate([jnp.where(lane < 64, rims, 0.0), none], axis=1)
            if j == 3:
                acc = acc + jnp.concatenate([none, jnp.where(lane < 64, 0.0, rims)], axis=1)
            mask = mbuf[pl.ds(4 * half, 4), :, pl.ds(256 * j, 256)].reshape(256, 256).astype(F32)
            voxels = (jnp.maximum(acc * gain4 + bias4, 0.0) * mask).astype(BF16)
            sums = sums + jnp.dot(voxels, hw_ref[pl.ds(256 * j, 256), :], preferred_element_type=F32)
        part[pl.ds(4 * half + 1, 4)] = sums.reshape(4, 64, 128)

    def sum_copy(target, source):
        return pltpu.make_async_remote_copy(
            src_ref=part.at[pl.ds(target * share + 1, share)],
            dst_ref=rbuf.at[source, pl.ds(1, share)],
            send_sem=sum_send.at[target],
            recv_sem=sum_recv.at[source],
            device_id={"slab": target},
            device_id_type=MESH,
        )

    def low_copy(target, a, source):
        return pltpu.make_async_remote_copy(
            src_ref=part.at[pl.ds(8 if a else target * share, 1)],
            dst_ref=rbuf.at[source, pl.ds(0, 1)],
            send_sem=low_send.at[target],
            recv_sem=low_recv.at[source],
            device_id={"strip": s + a, "slab": target},
            device_id_type=MESH,
        )

    def high_copy(target, a, source):
        return pltpu.make_async_remote_copy(
            src_ref=part.at[pl.ds(1 if a else target * share + share + 1, 1)],
            dst_ref=rbuf.at[source, pl.ds(share + 1, 1)],
            send_sem=high_send.at[target],
            recv_sem=high_recv.at[source],
            device_id={"strip": s + a, "slab": target},
            device_id_type=MESH,
        )

    def col_copy(side, a, target, source):
        return pltpu.make_async_remote_copy(
            src_ref=edge.at[side],
            dst_ref=cbuf.at[side, source, pl.ds(8 * (1 - a), 8)],
            send_sem=col_send.at[side, a + 1, target],
            recv_sem=col_recv.at[side, a + 1, source],
            device_id={
                "strip": s + a,
                "slab": target,
                "sub": u + 1 if side == 0 else u - 1,
            },
            device_id_type=MESH,
        )

    has_up = s < n_strip - 1
    has_down = s > 0
    last = n_slab - 1

    conv_half(1 - mine)
    for t in range(n_slab):

        @pl.when(t // (n_slab // 2) != mine)
        def _():
            sum_copy(t, l).start()

    conv_half(mine)

    edge[0] = part[pl.ds(1, 8), 56:64, :][:, 7, :]
    edge[1] = part[pl.ds(1, 8), 0:8, :][:, 0, :]

    for t in range(n_slab):

        @pl.when((l != t) & (t // (n_slab // 2) == mine))
        def _():
            sum_copy(t, l).start()

        if t > 0:

            @pl.when(l != t)
            def _():
                low_copy(t, 0, l).start()

        if t < last:

            @pl.when(l != t)
            def _():
                high_copy(t, 0, l).start()

    @pl.when(has_up)
    def _():
        low_copy(0, 1, l).start()

    @pl.when(has_down)
    def _():
        high_copy(last, -1, l).start()

    for side in range(2):

        @pl.when(sub_to[side])
        def _():
            for t in range(n_slab):
                col_copy(side, 0, t, l).start()

        @pl.when(sub_to[side] & has_up)
        def _():
            col_copy(side, 1, 0, l).start()

        @pl.when(sub_to[side] & has_down)
        def _():
            col_copy(side, -1, last, l).start()

    for source in range(n_slab):

        @pl.when(l != source)
        def _():
            sum_copy(0, source).wait_recv()

        @pl.when(((l > 0) & (l != source)) | ((l == 0) & has_down))
        def _():
            low_copy(0, 1, source).wait_recv()

        @pl.when(((l < last) & (l != source)) | ((l == last) & has_up))
        def _():
            high_copy(0, -1, source).wait_recv()

        for side in range(2):

            @pl.when(sub_from[side])
            def _():
                col_copy(side, 0, 0, source).wait_recv()

            @pl.when(sub_from[side] & (l == 0) & has_down)
            def _():
                col_copy(side, 1, 0, source).wait_recv()

            @pl.when(sub_from[side] & (l == last) & has_up)
            def _():
                col_copy(side, -1, 0, source).wait_recv()

    hb = hb_ref[...]
    first_x = s * 8 + l * share - 1

    col_x = lax.broadcasted_iota(jnp.int32, (24, 128), 0) + (s * 8 - 8)
    for side in range(2):
        col = cbuf[side, 0]
        for source in range(1, n_slab):
            col = col + cbuf[side, source]
        inside = (col_x >= 0) & (col_x < 8 * n_strip) & sub_from[side]
        hcol[side] = jnp.where(inside, jnp.maximum(col + hb, 0.0), 0.0)

    for i in range(share + 2):
        total = part[l * share + i]
        for source in range(n_slab):
            total = total + rbuf[source, i]
        total = jnp.maximum(total + hb, 0.0)
        if i == 0 or i == share + 1:
            row_ok = (first_x + i >= 0) & (first_x + i < 8 * n_strip)
            total = jnp.where(row_ok, total, 0.0)
        row_at = lax.broadcasted_iota(jnp.int32, total.shape, 0)
        before = hcol[0, pl.ds(7 + l * share + i, 1), :]
        after = hcol[1, pl.ds(7 + l * share + i, 1), :]
        bexp[i, :, pl.ds(0, 128)] = jnp.where(row_at == 0, before, pltpu.roll(total, 1, 0)).astype(
            BF16
        )
        bexp[i, :, pl.ds(128, 128)] = total.astype(BF16)
        bexp[i, :, pl.ds(256, 128)] = jnp.where(row_at == 63, after, pltpu.roll(total, 63, 0)).astype(
            BF16
        )

    pre = jnp.zeros((share * 64, bw_ref.shape[2]), F32)
    for dx in range(3):
        pre = pre + jnp.dot(
            bexp[pl.ds(dx, share)].reshape(share * 64, 384), bw_ref[dx], preferred_element_type=F32
        )
    hidden = jnp.maximum(pre * bgain_ref[...] + bbias_ref[...], 0.0).astype(BF16)
    maps = lax.dot_general(
        head_ref[...], hidden, (((1,), (1,)), ((), ())), preferred_element_type=F32
    )
    maps = maps + jnp.transpose(jnp.broadcast_to(headb_ref[...], (8, headb_ref.shape[1])))[:, 0:1]
    for i in range(share):
        out_ref[:, i, :] = maps[:, 64 * i : 64 * i + 64]

    for at, (a, b) in enumerate(DIRS):

        @pl.when(exists(a, b))
        def _():
            face_copy(at).wait_send()
            for side in range(2):

                @pl.when(sub_to[side])
                def _():
                    y_copy(side, at + 1).wait_send()

    for side in range(2):

        @pl.when(sub_to[side])
        def _():
            y_copy(side, 0).wait_send()
            for t in range(n_slab):
                col_copy(side, 0, t, l).wait_send()

        @pl.when(sub_to[side] & has_up)
        def _():
            col_copy(side, 1, 0, l).wait_send()

        @pl.when(sub_to[side] & has_down)
        def _():
            col_copy(side, -1, last, l).wait_send()

    for t in range(n_slab):

        @pl.when(l != t)
        def _():
            sum_copy(t, l).wait_send()
            if t > 0:
                low_copy(t, 0, l).wait_send()
            if t < last:
                high_copy(t, 0, l).wait_send()

    @pl.when(has_up)
    def _():
        low_copy(0, 1, l).wait_send()

    @pl.when(has_down)
    def _():
        high_copy(last, -1, l).wait_send()


def solution(mesh):
    n_strip, n_slab, n_sub = mesh.shape["strip"], mesh.shape["slab"], mesh.shape["sub"]
    share = 8 // n_slab

    def on_device(
        features,
        voxel_mask,
        block_pos,
        conv_weight,
        conv_gain,
        conv_bias,
        height_weight,
        height_bias,
        bev_weight,
        bev_gain,
        bev_bias,
        head_weight,
        head_bias,
    ):
        heads = head_weight.shape[1]
        chan_out = bev_weight.shape[3]
        vmem = pl.BlockSpec(memory_space=pltpu.VMEM)
        far = pl.BlockSpec(memory_space=pl.ANY)
        places = block_pos.reshape(12)
        operands = (
            features.reshape(12, 64, 512),
            voxel_mask.reshape(12, 8, 8, 8).transpose(1, 2, 3, 0).reshape(512, 12),
            places.reshape(1, 12),
            conv_weight.reshape(27, 64, 64),
            conv_gain.reshape(1, -1),
            conv_bias.reshape(1, -1),
            height_weight,
            height_bias.reshape(1, -1),
            bev_weight.reshape(3, -1, chan_out),
            bev_gain.reshape(1, -1),
            bev_bias.reshape(1, -1),
            head_weight.T,
            head_bias.reshape(1, -1),
        )
        out = pl.pallas_call(
            lambda *refs: body((n_strip, n_slab, n_sub), *refs),
            out_shape=jax.ShapeDtypeStruct((heads, share, 64), F32),
            in_specs=[pl.BlockSpec(memory_space=pltpu.SMEM)] + [far] * 13,
            out_specs=vmem,
            scratch_shapes=[pltpu.VMEM(each.shape, each.dtype) for each in operands]
            + [
                pltpu.VMEM((12, 64, 1280), BF16),
                pltpu.VMEM((12, 64, 1280), BF16),
                pltpu.VMEM((12, 64, 1280), BF16),
                pltpu.VMEM((2, 10, 16, 1280), BF16),
                pltpu.VMEM((16, 64, 512), F32),
                pltpu.VMEM((8, 64, 1024), BF16),
                pltpu.VMEM((9, 512, 256), BF16),
                pltpu.VMEM((9, 256, 128), BF16),
                pltpu.VMEM((10, 64, 256), BF16),
                pltpu.VMEM((10, 64, 256), BF16),
                pltpu.VMEM((10, 64, 256), BF16),
                pltpu.VMEM((4, 8, 64, 256), F32),
                pltpu.VMEM((10, 64, 128), F32),
                pltpu.VMEM((2, 8, 128), F32),
                pltpu.VMEM((n_slab, share + 2, 64, 128), F32),
                pltpu.VMEM((2, n_slab, 24, 128), F32),
                pltpu.VMEM((2, 24, 128), F32),
                pltpu.VMEM((share + 2, 64, 384), BF16),
                pltpu.SemaphoreType.DMA((13,)),
                pltpu.SemaphoreType.DMA((8,)),
                pltpu.SemaphoreType.DMA((8,)),
                pltpu.SemaphoreType.DMA((2, 9)),
                pltpu.SemaphoreType.DMA((2, 9)),
            ]
            + [pltpu.SemaphoreType.DMA((n_slab,))] * 6
            + [pltpu.SemaphoreType.DMA((2, 3, n_slab))] * 2,
            compiler_params=pltpu.CompilerParams(
                collective_id=0, has_side_effects=True, vmem_limit_bytes=60 * 2**20
            ),
        )(places, *operands)
        return out.transpose(1, 2, 0)

    in_specs = (
        P(("groups", "strip"), "sub", "slab", None, None, None, None),
        P(("groups", "strip"), "sub", "slab", None, None, None, None),
        P(("groups", "strip"), "sub", "slab", None),
        P(),
        P(),
        P(),
        P("slab", None),
        P(),
        P(),
        P(),
        P(),
        P(),
        P(),
    )
    out_specs = P(("groups", "strip", "slab"), "sub", None)
    return jax.shard_map(
        on_device, mesh=mesh, in_specs=in_specs, out_specs=out_specs, check_vma=False
    )
```

```python
import jax
import jax.numpy as jnp
from jax import lax
from jax.experimental import pallas as pl
from jax.experimental.pallas import tpu as pltpu
from jax.sharding import PartitionSpec as P

BY_DEV = 8
BZ_DEV = 2
MESH = pl.DeviceIdType.MESH
F32 = jnp.float32
BF16 = jnp.bfloat16

DIRS = [(a, b) for a in (-1, 0, 1) for b in (-1, 0, 1) if (a, b) != (0, 0)]
Y_DIRS = [(0, 0)] + DIRS


def body(
    sizes,
    pos_ref,
    feat_hbm,
    mask_hbm,
    posv_hbm,
    cw_hbm,
    gain_hbm,
    bias_hbm,
    hw_hbm,
    hb_hbm,
    bw_hbm,
    bgain_hbm,
    bbias_hbm,
    head_hbm,
    headb_hbm,
    out_ref,
    feat_ref,
    mask_ref,
    posv_ref,
    cw_ref,
    gain_ref,
    bias_ref,
    hw_ref,
    hb_ref,
    bw_ref,
    bgain_ref,
    bbias_ref,
    head_ref,
    headb_ref,
    xbuf,
    xm,
    xp,
    ybuf,
    wide,
    mbuf,
    band,
    zband,
    zbuf,
    zm,
    zp,
    accb,
    part,
    edge,
    rbuf,
    cbuf,
    hcol,
    bexp,
    in_sem,
    face_send,
    face_recv,
    y_send,
    y_recv,
    sum_send,
    sum_recv,
    low_send,
    low_recv,
    high_send,
    high_recv,
    col_send,
    col_recv,
):
    n_strip, n_slab, n_sub = sizes
    share = 8 // n_slab
    s = lax.axis_index("strip")
    l = lax.axis_index("slab")
    u = lax.axis_index("sub")

    fetched = (
        (posv_hbm, posv_ref),
        (mask_hbm, mask_ref),
        (feat_hbm, feat_ref),
        (cw_hbm, cw_ref),
        (gain_hbm, gain_ref),
        (bias_hbm, bias_ref),
        (hw_hbm, hw_ref),
        (hb_hbm, hb_ref),
        (bw_hbm, bw_ref),
        (bgain_hbm, bgain_ref),
        (bbias_hbm, bbias_ref),
        (head_hbm, head_ref),
        (headb_hbm, headb_ref),
    )
    fetches = [
        pltpu.make_async_copy(src, dst, in_sem.at[at]) for at, (src, dst) in enumerate(fetched)
    ]
    for fetch in fetches[:4]:
        fetch.start()

    for side in (0, 9, 10, 11):
        xbuf[side] = jnp.zeros((64, 1280), BF16)
        xm[side] = jnp.zeros((64, 1280), BF16)
        xp[side] = jnp.zeros((64, 1280), BF16)
    for low in (0, 1152):
        for each in (xm, xp):
            each[pl.ds(1, 8), :, pl.ds(low, 128)] = jnp.zeros((8, 64, 128), BF16)
    xbuf[pl.ds(1, 8), :, pl.ds(0, 128)] = jnp.zeros((8, 64, 128), BF16)
    xbuf[pl.ds(1, 8), :, pl.ds(1152, 128)] = jnp.zeros((8, 64, 128), BF16)
    ybuf[...] = jnp.zeros(ybuf.shape, BF16)
    rbuf[...] = jnp.zeros(rbuf.shape, F32)
    zbuf[...] = jnp.zeros(zbuf.shape, BF16)
    cbuf[...] = jnp.zeros(cbuf.shape, F32)
    part[...] = jnp.zeros(part.shape, F32)

    barrier = pltpu.get_barrier_semaphore()
    for a in (-1, 0, 1):

        @pl.when((s + a >= 0) & (s + a < n_strip))
        def _():
            for dl in range(n_slab):
                for du in range(n_sub):
                    if a == 0 and dl == 0 and du == 0:
                        continue
                    pl.semaphore_signal(
                        barrier,
                        inc=1,
                        device_id={
                            "strip": s + a,
                            "slab": lax.rem(l + dl, n_slab),
                            "sub": lax.rem(u + du, n_sub),
                        },
                        device_id_type=MESH,
                    )

    level_of = lax.rem(lax.broadcasted_iota(jnp.int32, (512, 512), 0), 8)
    chan_of = lax.broadcasted_iota(jnp.int32, (512, 512), 1) // 64
    spread = (level_of == chan_of).astype(F32).astype(BF16)
    own_col = lax.broadcasted_iota(jnp.int32, (64, 512), 1) // 8
    keep = (own_col == lax.broadcasted_iota(jnp.int32, (64, 512), 0)).astype(F32)
    fetches[0].wait()
    fetches[1].wait()
    places = lax.broadcasted_iota(jnp.int32, (16, 12), 0)
    pick = (places == posv_ref[...]).astype(F32).astype(BF16)
    by_place = lax.dot_general(
        pick,
        mask_ref[...].astype(F32).astype(BF16),
        (((1,), (1,)), ((), ())),
        preferred_element_type=F32,
    )
    rows_of = jnp.concatenate([(by_place[p : p + 1] * keep).astype(BF16) for p in range(16)], axis=0)
    wide[...] = jnp.dot(rows_of, spread, preferred_element_type=F32).reshape(16, 64, 512)

    def slot_at(place):
        slot = jnp.int32(0)
        for t in range(12):
            slot = jnp.where(pos_ref[t] == place, t, slot)
        return slot

    fetches[2].wait()
    for fetch in fetches[4:]:
        fetch.start()
    for pz in range(BZ_DEV):
        for pair in range(BY_DEV // 2):
            masks, blocks = [], []
            for half in range(2):
                place = (2 * pair + half) * BZ_DEV + pz
                mask = wide[place]
                masks.append(mask.reshape(8, 8, 512))
                blocks.append((feat_ref[slot_at(place)].astype(F32) * mask).reshape(8, 8, 512))
            rows = pl.ds(16 * pair, 16)
            mbuf[:, rows, pl.ds(512 * pz, 512)] = jnp.concatenate(masks, axis=1).astype(BF16)
            xbuf[pl.ds(1, 8), rows, pl.ds(128 + 512 * pz, 512)] = jnp.concatenate(
                blocks, axis=1
            ).astype(BF16)

    fetches[3].wait()

    def make_band(tap, carry):
        blank = jnp.zeros((64, 64), BF16)
        taps = [cw_ref[3 * tap + k] for k in range(3)]
        for e in range(8):
            cols = [taps[e - o - 1] if 0 <= e - o - 1 <= 2 else blank for o in range(4)]
            band[tap, pl.ds(64 * e, 64), :] = jnp.concatenate(cols, axis=1)
        low = jnp.concatenate([taps[0], blank], axis=1)
        high = jnp.concatenate([blank, taps[2]], axis=1)
        empty = jnp.zeros((64, 128), BF16)
        for e, rim in enumerate((empty, low, high, empty)):
            zband[tap, pl.ds(64 * e, 64), :] = rim
        return carry

    lax.fori_loop(0, 9, make_band, 0)

    def conv_own(j, sources):
        low = pl.multiple_of(256 * j, 256)
        taps = [(dx, dy, source) for dx in range(3) for dy, source in sources]
        windows = [
            source[pl.ds(dx, 8), :, pl.ds(low, 512)].reshape(512, 512) for dx, dy, source in taps
        ]
        weights = [band[3 * dx + dy] for dx, dy, source in taps]
        acc = jnp.dot(
            jnp.concatenate(windows, axis=1),
            jnp.concatenate(weights, axis=0),
            preferred_element_type=F32,
        )
        return acc.reshape(8, 64, 256)

    def conv_middle(j, carry):
        accb[j] = conv_own(j, ((1, xbuf),))
        return carry

    def conv_sides(j, carry):
        accb[j] += conv_own(j, ((0, xm), (2, xp)))
        return carry

    lax.fori_loop(0, 2, conv_middle, 0)

    strips_near = (s > 0).astype(jnp.int32) + (s < n_strip - 1).astype(jnp.int32) + 1
    pl.semaphore_wait(barrier, strips_near * (n_slab * n_sub) - 1)

    def exists(a, b):
        return (s + a >= 0) & (s + a < n_strip) & (l + b >= 0) & (l + b < n_slab)

    sub_to = (u < n_sub - 1, u > 0)
    sub_from = (u > 0, u < n_sub - 1)

    def ranges(a, b):
        src_x, dst_x = {-1: ((1, 1), (9, 1)), 0: ((1, 8), (1, 8)), 1: ((8, 1), (0, 1))}[a]
        src_z, dst_z = {
            -1: ((128, 128), (1152, 128)),
            0: ((128, 1024), (128, 1024)),
            1: ((1024, 128), (0, 128)),
        }[b]
        return pl.ds(*src_x), pl.ds(*dst_x), pl.ds(*src_z), pl.ds(*dst_z)

    def face_copy(at):
        a, b = DIRS[at]
        src_x, dst_x, src_z, dst_z = ranges(a, b)
        if b == 0:
            target = xbuf.at[pl.ds(11 if a < 0 else 10, 1), :, dst_z]
        else:
            target = zbuf.at[dst_x, :, pl.ds(128 if b < 0 else 0, 128)]
        return pltpu.make_async_remote_copy(
            src_ref=xbuf.at[src_x, :, src_z],
            dst_ref=target,
            send_sem=face_send.at[at],
            recv_sem=face_recv.at[at],
            device_id={"strip": s + a, "slab": l + b},
            device_id_type=MESH,
        )

    def y_copy(side, at):
        a, b = Y_DIRS[at]
        src_x, dst_x, src_z, dst_z = ranges(a, b)
        return pltpu.make_async_remote_copy(
            src_ref=xbuf.at[src_x, pl.ds(48 if side == 0 else 0, 16), src_z],
            dst_ref=ybuf.at[side, dst_x, :, dst_z],
            send_sem=y_send.at[side, at],
            recv_sem=y_recv.at[side, at],
            device_id={
                "strip": s + a,
                "slab": l + b,
                "sub": u + 1 if side == 0 else u - 1,
            },
            device_id_type=MESH,
        )

    for side in range(2):

        @pl.when(sub_to[side])
        def _():
            y_copy(side, 0).start()

    for at, (a, b) in enumerate(DIRS):

        @pl.when(exists(a, b))
        def _():
            face_copy(at).start()
            for side in range(2):

                @pl.when(sub_to[side])
                def _():
                    y_copy(side, at + 1).start()

    lax.fori_loop(2, 4, conv_middle, 0)

    for fetch in fetches[4:]:
        fetch.wait()

    for side in range(2):

        @pl.when(sub_from[side])
        def _():
            y_copy(side, 0).wait_recv()

    def shift_rows(x, low, width):
        lanes = pl.ds(low, width)
        rows = xbuf[x, :, lanes].astype(F32)
        row_at = lax.broadcasted_iota(jnp.int32, rows.shape, 0)
        before = ybuf[0, x, :, lanes].astype(F32)[15:16]
        after = ybuf[1, x, :, lanes].astype(F32)[0:1]
        xm[x, :, lanes] = jnp.where(row_at == 0, before, pltpu.roll(rows, 1, 0)).astype(BF16)
        xp[x, :, lanes] = jnp.where(row_at == 63, after, pltpu.roll(rows, 63, 0)).astype(BF16)

    def shift_own(x, carry):
        shift_rows(x, 128, 1024)
        return carry

    lax.fori_loop(1, 9, shift_own, 0)

    gain4 = jnp.concatenate([gain_ref[...]] * 4, axis=1)
    bias4 = jnp.concatenate([bias_ref[...]] * 4, axis=1)

    lax.fori_loop(0, 4, conv_sides, 0)

    for at, (a, b) in enumerate(DIRS):

        @pl.when(exists(-a, -b))
        def _():
            face_copy(at).wait_recv()
            for side in range(2):

                @pl.when(sub_from[side])
                def _():
                    y_copy(side, at + 1).wait_recv()

    def shifted(rows, before, after):
        row_at = lax.broadcasted_iota(jnp.int32, rows.shape, 0)
        up = jnp.where(row_at == 0, before, pltpu.roll(rows, 1, 0)).astype(BF16)
        down = jnp.where(row_at == 63, after, pltpu.roll(rows, 63, 0)).astype(BF16)
        return up, down

    def shift_ends(at, carry):
        lanes = pl.ds(128, 1024)
        xm[10 + at, :, lanes], xp[10 + at, :, lanes] = shifted(
            xbuf[10 + at, :, lanes].astype(F32),
            ybuf[0, 9 * at, :, lanes].astype(F32)[15:16],
            ybuf[1, 9 * at, :, lanes].astype(F32)[0:1],
        )
        return carry

    lax.fori_loop(0, 2, shift_ends, 0)

    def shift_rims(x, carry):
        before, after = [
            jnp.concatenate(
                [ybuf[side, x, :, pl.ds(low, 128)].astype(F32) for low in (0, 1152)], axis=1
            )
            for side in range(2)
        ]
        zm[x], zp[x] = shifted(zbuf[x].astype(F32), before[15:16], after[0:1])
        return carry

    lax.fori_loop(0, 10, shift_rims, 0)

    mine = l // (n_slab // 2)

    def conv_half(half):
        beyond = jnp.zeros((256, 256), F32)
        for dy, source in enumerate((xm, xbuf, xp)):
            window = jnp.concatenate([source[10 + half, :, pl.ds(256 * j, 512)] for j in range(4)], axis=0)
            beyond = beyond + jnp.dot(window, band[6 * half + dy], preferred_element_type=F32)
        accb[:, 7 * half] += beyond.reshape(4, 64, 256)
        rims = jnp.zeros((256, 128), F32)
        for dx in range(3):
            for dy, source in enumerate((zm, zbuf, zp)):
                window = source[pl.ds(4 * half + dx, 4)].reshape(256, 256)
                rims = rims + jnp.dot(window, zband[3 * dx + dy], preferred_element_type=F32)
        lane = lax.broadcasted_iota(jnp.int32, rims.shape, 1)
        none = jnp.zeros_like(rims)
        sums = jnp.zeros((256, 128), F32)
        for j in range(4):
            acc = accb[j, pl.ds(4 * half, 4)].reshape(256, 256)
            if j == 0:
                acc = acc + jnp.concatenate([jnp.where(lane < 64, rims, 0.0), none], axis=1)
            if j == 3:
                acc = acc + jnp.concatenate([none, jnp.where(lane < 64, 0.0, rims)], axis=1)
            mask = mbuf[pl.ds(4 * half, 4), :, pl.ds(256 * j, 256)].reshape(256, 256).astype(F32)
            voxels = (jnp.maximum(acc * gain4 + bias4, 0.0) * mask).astype(BF16)
            sums = sums + jnp.dot(voxels, hw_ref[pl.ds(256 * j, 256), :], preferred_element_type=F32)
        part[pl.ds(4 * half + 1, 4)] = sums.reshape(4, 64, 128)

    def sum_copy(target, source):
        return pltpu.make_async_remote_copy(
            src_ref=part.at[pl.ds(target * share + 1, share)],
            dst_ref=rbuf.at[source, pl.ds(1, share)],
            send_sem=sum_send.at[target],
            recv_sem=sum_recv.at[source],
            device_id={"slab": target},
            device_id_type=MESH,
        )

    def low_copy(target, a, source):
        return pltpu.make_async_remote_copy(
            src_ref=part.at[pl.ds(8 if a else target * share, 1)],
            dst_ref=rbuf.at[source, pl.ds(0, 1)],
            send_sem=low_send.at[target],
            recv_sem=low_recv.at[source],
            device_id={"strip": s + a, "slab": target},
            device_id_type=MESH,
        )

    def high_copy(target, a, source):
        return pltpu.make_async_remote_copy(
            src_ref=part.at[pl.ds(1 if a else target * share + share + 1, 1)],
            dst_ref=rbuf.at[source, pl.ds(share + 1, 1)],
            send_sem=high_send.at[target],
            recv_sem=high_recv.at[source],
            device_id={"strip": s + a, "slab": target},
            device_id_type=MESH,
        )

    def col_copy(side, a, target, source):
        return pltpu.make_async_remote_copy(
            src_ref=edge.at[side],
            dst_ref=cbuf.at[side, source, pl.ds(8 * (1 - a), 8)],
            send_sem=col_send.at[side, a + 1, target],
            recv_sem=col_recv.at[side, a + 1, source],
            device_id={
                "strip": s + a,
                "slab": target,
                "sub": u + 1 if side == 0 else u - 1,
            },
            device_id_type=MESH,
        )

    has_up = s < n_strip - 1
    has_down = s > 0
    last = n_slab - 1

    conv_half(1 - mine)
    for t in range(n_slab):

        @pl.when(t // (n_slab // 2) != mine)
        def _():
            sum_copy(t, l).start()

    conv_half(mine)

    edge[0] = part[pl.ds(1, 8), 56:64, :][:, 7, :]
    edge[1] = part[pl.ds(1, 8), 0:8, :][:, 0, :]

    for t in range(n_slab):

        @pl.when((l != t) & (t // (n_slab // 2) == mine))
        def _():
            sum_copy(t, l).start()

        if t > 0:

            @pl.when(l != t)
            def _():
                low_copy(t, 0, l).start()

        if t < last:

            @pl.when(l != t)
            def _():
                high_copy(t, 0, l).start()

    @pl.when(has_up)
    def _():
        low_copy(0, 1, l).start()

    @pl.when(has_down)
    def _():
        high_copy(last, -1, l).start()

    for side in range(2):

        @pl.when(sub_to[side])
        def _():
            for t in range(n_slab):
                col_copy(side, 0, t, l).start()

        @pl.when(sub_to[side] & has_up)
        def _():
            col_copy(side, 1, 0, l).start()

        @pl.when(sub_to[side] & has_down)
        def _():
            col_copy(side, -1, last, l).start()

    for source in range(n_slab):

        @pl.when(l != source)
        def _():
            sum_copy(0, source).wait_recv()

        @pl.when(((l > 0) & (l != source)) | ((l == 0) & has_down))
        def _():
            low_copy(0, 1, source).wait_recv()

        @pl.when(((l < last) & (l != source)) | ((l == last) & has_up))
        def _():
            high_copy(0, -1, source).wait_recv()

        for side in range(2):

            @pl.when(sub_from[side])
            def _():
                col_copy(side, 0, 0, source).wait_recv()

            @pl.when(sub_from[side] & (l == 0) & has_down)
            def _():
                col_copy(side, 1, 0, source).wait_recv()

            @pl.when(sub_from[side] & (l == last) & has_up)
            def _():
                col_copy(side, -1, 0, source).wait_recv()

    hb = hb_ref[...]
    first_x = s * 8 + l * share - 1

    col_x = lax.broadcasted_iota(jnp.int32, (24, 128), 0) + (s * 8 - 8)
    for side in range(2):
        col = cbuf[side, 0]
        for source in range(1, n_slab):
            col = col + cbuf[side, source]
        inside = (col_x >= 0) & (col_x < 8 * n_strip) & sub_from[side]
        hcol[side] = jnp.where(inside, jnp.maximum(col + hb, 0.0), 0.0)

    for i in range(share + 2):
        total = part[l * share + i]
        for source in range(n_slab):
            total = total + rbuf[source, i]
        total = jnp.maximum(total + hb, 0.0)
        if i == 0 or i == share + 1:
            row_ok = (first_x + i >= 0) & (first_x + i < 8 * n_strip)
            total = jnp.where(row_ok, total, 0.0)
        row_at = lax.broadcasted_iota(jnp.int32, total.shape, 0)
        before = hcol[0, pl.ds(7 + l * share + i, 1), :]
        after = hcol[1, pl.ds(7 + l * share + i, 1), :]
        bexp[i, :, pl.ds(0, 128)] = jnp.where(row_at == 0, before, pltpu.roll(total, 1, 0)).astype(
            BF16
        )
        bexp[i, :, pl.ds(128, 128)] = total.astype(BF16)
        bexp[i, :, pl.ds(256, 128)] = jnp.where(row_at == 63, after, pltpu.roll(total, 63, 0)).astype(
            BF16
        )

    pre = jnp.zeros((share * 64, bw_ref.shape[2]), F32)
    for dx in range(3):
        pre = pre + jnp.dot(
            bexp[pl.ds(dx, share)].reshape(share * 64, 384), bw_ref[dx], preferred_element_type=F32
        )
    hidden = jnp.maximum(pre * bgain_ref[...] + bbias_ref[...], 0.0).astype(BF16)
    maps = lax.dot_general(
        head_ref[...], hidden, (((1,), (1,)), ((), ())), preferred_element_type=F32
    )
    maps = maps + jnp.transpose(jnp.broadcast_to(headb_ref[...], (8, headb_ref.shape[1])))[:, 0:1]
    for i in range(share):
        out_ref[:, i, :] = maps[:, 64 * i : 64 * i + 64]

    for at, (a, b) in enumerate(DIRS):

        @pl.when(exists(a, b))
        def _():
            face_copy(at).wait_send()
            for side in range(2):

                @pl.when(sub_to[side])
                def _():
                    y_copy(side, at + 1).wait_send()

    for side in range(2):

        @pl.when(sub_to[side])
        def _():
            y_copy(side, 0).wait_send()
            for t in range(n_slab):
                col_copy(side, 0, t, l).wait_send()

        @pl.when(sub_to[side] & has_up)
        def _():
            col_copy(side, 1, 0, l).wait_send()

        @pl.when(sub_to[side] & has_down)
        def _():
            col_copy(side, -1, last, l).wait_send()

    for t in range(n_slab):

        @pl.when(l != t)
        def _():
            sum_copy(t, l).wait_send()
            if t > 0:
                low_copy(t, 0, l).wait_send()
            if t < last:
                high_copy(t, 0, l).wait_send()

    @pl.when(has_up)
    def _():
        low_copy(0, 1, l).wait_send()

    @pl.when(has_down)
    def _():
        high_copy(last, -1, l).wait_send()


def solution(mesh):
    n_strip, n_slab, n_sub = mesh.shape["strip"], mesh.shape["slab"], mesh.shape["sub"]
    share = 8 // n_slab

    def on_device(
        features,
        voxel_mask,
        block_pos,
        conv_weight,
        conv_gain,
        conv_bias,
        height_weight,
        height_bias,
        bev_weight,
        bev_gain,
        bev_bias,
        head_weight,
        head_bias,
    ):
        heads = head_weight.shape[1]
        chan_out = bev_weight.shape[3]
        vmem = pl.BlockSpec(memory_space=pltpu.VMEM)
        far = pl.BlockSpec(memory_space=pl.ANY)
        places = block_pos.reshape(12)
        operands = (
            features.reshape(12, 64, 512),
            voxel_mask.reshape(12, 8, 8, 8).transpose(1, 2, 3, 0).reshape(512, 12),
            places.reshape(1, 12),
            conv_weight.reshape(27, 64, 64),
            conv_gain.reshape(1, -1),
            conv_bias.reshape(1, -1),
            height_weight,
            height_bias.reshape(1, -1),
            bev_weight.reshape(3, -1, chan_out),
            bev_gain.reshape(1, -1),
            bev_bias.reshape(1, -1),
            head_weight.T,
            head_bias.reshape(1, -1),
        )
        out = pl.pallas_call(
            lambda *refs: body((n_strip, n_slab, n_sub), *refs),
            out_shape=jax.ShapeDtypeStruct((heads, share, 64), F32),
            in_specs=[pl.BlockSpec(memory_space=pltpu.SMEM)] + [far] * 13,
            out_specs=vmem,
            scratch_shapes=[pltpu.VMEM(each.shape, each.dtype) for each in operands]
            + [
                pltpu.VMEM((12, 64, 1280), BF16),
                pltpu.VMEM((12, 64, 1280), BF16),
                pltpu.VMEM((12, 64, 1280), BF16),
                pltpu.VMEM((2, 10, 16, 1280), BF16),
                pltpu.VMEM((16, 64, 512), F32),
                pltpu.VMEM((8, 64, 1024), BF16),
                pltpu.VMEM((9, 512, 256), BF16),
                pltpu.VMEM((9, 256, 128), BF16),
                pltpu.VMEM((10, 64, 256), BF16),
                pltpu.VMEM((10, 64, 256), BF16),
                pltpu.VMEM((10, 64, 256), BF16),
                pltpu.VMEM((4, 8, 64, 256), F32),
                pltpu.VMEM((10, 64, 128), F32),
                pltpu.VMEM((2, 8, 128), F32),
                pltpu.VMEM((n_slab, share + 2, 64, 128), F32),
                pltpu.VMEM((2, n_slab, 24, 128), F32),
                pltpu.VMEM((2, 24, 128), F32),
                pltpu.VMEM((share + 2, 64, 384), BF16),
                pltpu.SemaphoreType.DMA((13,)),
                pltpu.SemaphoreType.DMA((8,)),
                pltpu.SemaphoreType.DMA((8,)),
                pltpu.SemaphoreType.DMA((2, 9)),
                pltpu.SemaphoreType.DMA((2, 9)),
            ]
            + [pltpu.SemaphoreType.DMA((n_slab,))] * 6
            + [pltpu.SemaphoreType.DMA((2, 3, n_slab))] * 2,
            compiler_params=pltpu.CompilerParams(
                collective_id=0, has_side_effects=True, vmem_limit_bytes=60 * 2**20
            ),
        )(places, *operands)
        return out.transpose(1, 2, 0)

    in_specs = (
        P(("groups", "strip"), "sub", "slab", None, None, None, None),
        P(("groups", "strip"), "sub", "slab", None, None, None, None),
        P(("groups", "strip"), "sub", "slab", None),
        P(),
        P(),
        P(),
        P("slab", None),
        P(),
        P(),
        P(),
        P(),
        P(),
        P(),
    )
    out_specs = P(("groups", "strip", "slab"), "sub", None)
    return jax.shard_map(
        on_device, mesh=mesh, in_specs=in_specs, out_specs=out_specs, check_vma=False
    )
```
